32 devices in a mesh: gx: 8 (over z, x), gy: 2 (over core), gz: 2 (over y).
Axes of the slice: x: 2, y: 2, z: 4, core: 2. Of those that a mesh axis runs over, the one named last changes fastest.
Arguments:
- populations: float32 [19, 32, 32, 512], P(None, 'gx', 'gz', 'gy'), may hold values from 0.01 to 0.21
- nozzle_mask: int32 [32, 512], P('gx', 'gy'), may hold values 0 or 1
- wall_type: int32 [32, 512], P('gx', 'gy'), may hold values from 0 to 1
- solid_temp: float32 [32, 64, 512], P('gx', None, ('gy', 'gz')), may hold values from -6 to 6
- diffusion: float32 [32, 64, 512], P('gx', None, ('gy', 'gz')), may hold values from 0.3 to 3
- heat_load: float32 [32, 512], P('gx', ('gy', 'gz')), may hold values from 0.2 to 2
- coolant_temp: float32 [32, 512], P('gx', ('gy', 'gz')), may hold values from -2 to 0
Outputs:
- populations_next: float32 [19, 32, 32, 512], P(None, 'gx', 'gz', 'gy')
- solid_next: float32 [32, 64, 512], P('gx', None, ('gy', 'gz'))
The draws below stay inside these ranges and needn't reach their ends.
Inputs may be any that keep to these rules, and one draw needn't show every extreme that they name: `nozzle_mask`: 1 marks a nozzle opening; it takes precedence over wall_type. `wall_type`: 1 marks an outlet cell of the plate, 0 a closed plate cell.
All inputs are finite; a program needn't handle non-finite values. No bound on the sum of `nozzle_mask` on one device may be relied on, other than what follows from the above.
Results may differ from the reference program's by a relative error of at most 0.0001.
Values sent between devices are 32-bit elements; how exact they have to be, the bound alone decides.
A program may use at most 64 MiB of HBM per device.

```python
import math
import jax
import jax.numpy as jnp
import numpy as np
from jax import lax

Q = 19
SZ = 64
NX = 32
NY = 512
NZ = 32


def set_ends(values, key, least, high):
    spot = [jax.random.randint(jax.random.fold_in(key, axis), (), 0, length) for axis, length in enumerate(values.shape)]
    longest = values.shape.index(max(values.shape))
    next_to = spot[:longest] + [(spot[longest] + 1) % values.shape[longest]] + spot[longest + 1:]
    return values.at[tuple(spot)].set(least).at[tuple(next_to)].set(high)


def block_levels(stream_key, dims, shards, smallest, high):
    factor_of = 1.0
    for position, shards_of in shards:
        steps = jax.random.uniform(jax.random.fold_in(jax.random.fold_in(stream_key, 6), position), (shards_of,), jnp.float32, smallest / len(shards), high / len(shards))
        factor_of = factor_of * jnp.repeat(jnp.exp(steps), dims[position] // shards_of).reshape((-1,) + (1,) * (len(dims) - 1 - position))
    return factor_of


def centred(rng, shape, scale, most, pieces=(), held_as=jnp.bfloat16):
    entries = jax.random.normal(rng, shape, jnp.float32) * scale
    if len(pieces) > 0:
        entries = block_levels(rng, shape, pieces, -0.22, 0.18) * entries
    return jnp.clip(entries, min=-most, max=most).astype(held_as)


def setup_inputs(seed: int = 0) -> dict:
    keys = jax.random.split(jax.random.key(seed), 8)
    populations = jnp.clip(0.01 + 0.19999999 * jax.random.uniform(keys[0], (Q, NX, NZ, NY), jnp.float32) ** block_levels(keys[0], (Q, NX, NZ, NY), ((1, 8), (2, 2), (3, 2)), -0.2, 0.2), 0.01, 0.21)
    nozzle_mask = set_ends((jax.random.randint(keys[1], (NX, NY), 0, 4) < 1).astype(jnp.int32), jax.random.fold_in(keys[1], 1), 0, 1)
    wall_type = set_ends(jax.random.randint(keys[2], (NX, NY), 0, 2), jax.random.fold_in(keys[2], 1), 0, 1).astype(jnp.int32)
    solid_temp = centred(keys[3], (NX, SZ, NY), 1.0, 6.0, ((0, 8), (2, 4)), jnp.float32)
    diffusion = jnp.clip(jnp.exp(math.log(3.0) - 2.3025851 * jax.random.uniform(keys[4], (NX, SZ, NY), jnp.float32) ** block_levels(keys[4], (NX, SZ, NY), ((0, 8), (2, 4)), -0.2, 0.2)), 0.3, 3.0)
    heat_load = jnp.clip(jnp.exp(math.log(2.0) - 2.3025851 * jax.random.uniform(keys[5], (NX, NY), jnp.float32) ** block_levels(keys[5], (NX, NY), ((0, 8), (1, 4)), -0.2, 0.2)), 0.2, 2.0)
    coolant_temp = jnp.clip(-2.0 + 2.0 * jax.random.uniform(keys[6], (NX, NY), jnp.float32) ** block_levels(keys[6], (NX, NY), ((0, 8), (1, 4)), -0.2, 0.2), -2.0, 0.0)
    return dict(populations=populations, nozzle_mask=nozzle_mask, wall_type=wall_type, solid_temp=solid_temp, diffusion=diffusion, heat_load=heat_load, coolant_temp=coolant_temp)


JET_SPEED = 0.1
H_BASE = 0.5
H_GAIN = 40.0
SHEAR_RATE = 1.6
ODD_RATE = 1.2
EVEN_RATE = 1.4

def velocity_table():
    return np.array([[0, 0, 0], [1, 0, 0], [-1, 0, 0], [0, 1, 0], [0, -1, 0], [0, 0, 1], [0, 0, -1], [1, 1, 0], [-1, -1, 0], [1, -1, 0], [-1, 1, 0], [1, 0, 1], [-1, 0, -1], [1, 0, -1], [-1, 0, 1], [0, 1, 1], [0, -1, -1], [0, 1, -1], [0, -1, 1]], dtype=np.int32)

def weight_table():
    return np.array([1.0 / 3.0] + [1.0 / 18.0] * 6 + [1.0 / 36.0] * 12, dtype=np.float32)

def opposite_of(member):
    table = velocity_table()
    for other in range(table.shape[0]):
        if np.all(table[other] == -table[member]):
            return other
    return member

def relax_table():
    table = velocity_table().astype(np.float32)
    comp_a = table[:, 0]
    comp_b = table[:, 1]
    comp_c = table[:, 2]
    monomials = [comp_a * 0.0 + 1.0, comp_a, comp_b, comp_c, comp_a * comp_a, comp_b * comp_b, comp_c * comp_c, comp_a * comp_b, comp_b * comp_c, comp_a * comp_c, comp_a * comp_c * comp_c, comp_a * comp_b * comp_b, comp_c * comp_a * comp_a, comp_c * comp_b * comp_b, comp_b * comp_a * comp_a, comp_b * comp_c * comp_c, comp_a * comp_a * comp_c * comp_c, comp_a * comp_a * comp_b * comp_b, comp_c * comp_c * comp_b * comp_b]
    rates = np.array([0.0] * 4 + [SHEAR_RATE] * 6 + [ODD_RATE] * 6 + [EVEN_RATE] * 3, dtype=np.float32)
    ortho = []
    for monomial in monomials:
        vector = monomial.copy()
        for earlier in ortho:
            vector = vector - np.dot(earlier, vector) * earlier
        ortho.append(vector / np.sqrt(np.dot(vector, vector)))
    gram = np.stack(ortho)
    return (gram.T @ (rates[:, None] * gram)).astype(np.float32)

def collide(pops):
    table = jnp.asarray(velocity_table().astype(np.float32))
    weights = jnp.asarray(weight_table())
    density = lax.optimization_barrier(jnp.sum(pops, axis=0))
    momentum = jnp.einsum('qc,qxzy->cxzy', table, pops, precision=lax.Precision.HIGHEST)
    velocity = momentum / density[None]
    project = jnp.einsum('qc,cxzy->qxzy', table, velocity, precision=lax.Precision.HIGHEST)
    square = lax.optimization_barrier(jnp.sum(velocity * velocity, axis=0))
    equil = weights[:, None, None, None] * density[None] * (1.0 + 3.0 * project + 4.5 * project * project - 1.5 * square[None])
    relaxed = jnp.einsum('pq,qxzy->pxzy', jnp.asarray(relax_table()), pops - equil, precision=lax.Precision.HIGHEST)
    return (pops - relaxed, density, velocity)

def wall_coefficient(density_plane, velocity_plane):
    return H_BASE + H_GAIN * lax.optimization_barrier(jnp.sum(velocity_plane * velocity_plane, axis=0))

def apply_walls(moved, post, nozzle, outlet_kind, at_bottom, at_top):
    table = velocity_table()
    weights = weight_table()
    layers = []
    for member in range(table.shape[0]):
        layer = moved[member]
        other = opposite_of(member)
        if table[member, 2] > 0:
            bottom_value = post[other][:, 0, :]
            layer = layer.at[:, 0, :].set(jnp.where(at_bottom, bottom_value, layer[:, 0, :]))
        if table[member, 2] < 0:
            closed_value = post[other][:, -1, :]
            inlet_value = closed_value + 6.0 * float(weights[member]) * JET_SPEED
            outlet_value = post[member][:, -1, :]
            top_value = jnp.where(nozzle == 1, inlet_value, jnp.where(outlet_kind == 1, outlet_value, closed_value))
            layer = layer.at[:, -1, :].set(jnp.where(at_top, top_value, layer[:, -1, :]))
        layers.append(layer)
    return jnp.stack(layers)

def sweep_core(temp, cond, told, load, heat, coolant, neighbours):
    numer = told
    denom = jnp.ones_like(told)
    for near_temp, near_cond in neighbours:
        link = 0.5 * (cond + near_cond)
        numer = numer + link * near_temp
        denom = denom + link
    link = 0.5 * (cond[:, 1:] + cond[:, :-1])
    edge = jnp.zeros_like(cond[:, :1])
    numer = numer + jnp.concatenate([link * temp[:, 1:], edge], axis=1)
    denom = denom + jnp.concatenate([link, edge], axis=1)
    numer = numer + jnp.concatenate([edge, link * temp[:, :-1]], axis=1)
    denom = denom + jnp.concatenate([edge, link], axis=1)
    numer = numer.at[:, 0].add(load)
    numer = numer.at[:, -1].add(heat * coolant)
    denom = denom.at[:, -1].add(heat)
    return numer / denom

def rolled(temp, cond):
    result = []
    for shift_by, axis_id in ((1, 0), (-1, 0), (1, 2), (-1, 2)):
        result.append((jnp.roll(temp, shift_by, axis_id), jnp.roll(cond, shift_by, axis_id)))
    return result

def reference(populations, nozzle_mask, wall_type, solid_temp, diffusion, heat_load, coolant_temp):
    post, density, velocity = collide(populations)
    table = velocity_table()
    moved = jnp.stack([jnp.roll(post[member], (int(table[member, 0]), int(table[member, 2]), int(table[member, 1])), (0, 1, 2)) for member in range(table.shape[0])])
    populations_next = apply_walls(moved, post, nozzle_mask, wall_type, True, True)
    heat = wall_coefficient(density[:, 0, :], velocity[:, :, 0, :])
    first = sweep_core(solid_temp, diffusion, solid_temp, heat_load, heat, coolant_temp, rolled(solid_temp, diffusion))
    solid_next = sweep_core(first, diffusion, solid_temp, heat_load, heat, coolant_temp, rolled(first, diffusion))
    return (populations_next, solid_next)
```

```python
import functools
import jax
import jax.numpy as jnp
import numpy as np
from jax import lax
from jax.experimental import pallas as pl
from jax.experimental.pallas import tpu as pltpu
from jax.sharding import PartitionSpec as P

JET_SPEED = 0.1
H_BASE = 0.5
H_GAIN = 40.0
LANES = 128
ROWS = 8
MESH = pl.DeviceIdType.MESH

VELOCITIES = [
    (0, 0, 0),
    (1, 0, 0), (-1, 0, 0), (0, 1, 0), (0, -1, 0), (0, 0, 1), (0, 0, -1),
    (1, 1, 0), (-1, -1, 0), (1, -1, 0), (-1, 1, 0),
    (1, 0, 1), (-1, 0, -1), (1, 0, -1), (-1, 0, 1),
    (0, 1, 1), (0, -1, -1), (0, 1, -1), (0, -1, 1),
]
COUNT = len(VELOCITIES)
WEIGHTS = [1.0 / 3.0] + [1.0 / 18.0] * 6 + [1.0 / 36.0] * 12
INDEX = {velocity: member for member, velocity in enumerate(VELOCITIES)}
OPPOSITE = [INDEX[(-a, -b, -c)] for a, b, c in VELOCITIES]
ORDER = [i for s in (1, -1, 0) for i in range(COUNT) if VELOCITIES[i][0] == s]
SLOT = {member: place for place, member in enumerate(ORDER)}
FACE = sum(1 for v in VELOCITIES if v[0] == 1)
ACROSS = [(0, 0), (1, 0), (-1, 0), (0, 1), (0, -1)]


def collide(f):
    s = {i: f[i] + f[i + 1] for i in range(1, COUNT, 2)}
    d = {i: f[i] - f[i + 1] for i in range(1, COUNT, 2)}
    jx = (d[1] + d[7]) + (d[9] + d[11]) + d[13]
    jy = (d[3] + d[7]) + (d[15] - d[9]) + d[17]
    jz = (d[5] + d[11]) + (d[15] - d[13]) - d[17]
    sxy, sxz, syz = s[7] + s[9], s[11] + s[13], s[15] + s[17]
    rho = f[0] + (s[1] + s[3] + s[5]) + (sxy + sxz + syz)
    inv = 1.0 / rho
    ux, uy, uz = jx * inv, jy * inv, jz * inv
    px, py, pz = jx * ux, jy * uy, jz * uz
    p = px + py + pz
    base = rho - 1.5 * p
    hxy, hxz, hyz = px + py, px + pz, py + pz
    c4 = 4.0 * f[0] - base
    qxy = c4 + sxy - 2.0 * (s[1] + s[3]) + 0.5 * hxy
    qxz = c4 + sxz - 2.0 * (s[1] + s[5]) + 0.5 * hxz
    qyz = c4 + syz - 2.0 * (s[3] + s[5]) + 0.5 * hyz
    mean = (qxy + qxz + qyz) * (2.0 / 7.0)
    txy, txz, tyz = ((q - mean) * (0.2 / 12.0) for q in (qxy, qxz, qyz))
    post = [None] * COUNT
    post[0] = (1.6 / 3.0) * base - 0.6 * f[0] + 4.0 * (txy + txz + tyz)
    axis_base = (1.6 / 18.0) * base
    for i, pp, tt, j in ((1, px, txy + txz, jx), (3, py, txy + tyz, jy), (5, pz, txz + tyz, jz)):
        even = axis_base + 0.4 * pp - 0.3 * s[i] - 2.0 * tt
        odd = 0.2 * j - 0.1 * d[i]
        post[i], post[i + 1] = even + odd, even - odd
    diag_base = (1.6 / 36.0) * base
    for i, hh, tt, j, k, u in (
        (7, hxy, txy, jx, jy, uy), (11, hxz, txz, jx, jz, uz), (15, hyz, tyz, jy, jz, uz)
    ):
        both = diag_base + 0.2 * hh + tt
        cross = 0.4 * (j * u)
        even = both + cross - 0.3 * s[i]
        odd = 0.1 * (j + k - d[i])
        post[i], post[i + 1] = even + odd, even - odd
        even = both - cross - 0.3 * s[i + 2]
        odd = 0.1 * (j - k - d[i + 2])
        post[i + 2], post[i + 3] = even + odd, even - odd
    return post, p * inv


def lanes_like(shape):
    return lax.broadcasted_iota(jnp.int32, shape, len(shape) - 1)


def rows_like(shape):
    return lax.broadcasted_iota(jnp.int32, shape, len(shape) - 2)


def turned(value, shift, axis):
    shift = shift % value.shape[axis]
    return value if shift == 0 else pltpu.roll(value, shift, axis)


def edge_pack(tiles, last):
    lane = lanes_like((ROWS, LANES))
    packed = jnp.zeros((ROWS, LANES), jnp.float32)
    for k, tile in enumerate(tiles):
        packed = jnp.where(lane == k, turned(tile, k + 1 if last else k, 1), packed)
    return packed


def edge_column(packed, places, last):
    return jnp.concatenate(
        [turned(packed, (LANES - 1 if last else 0) - k, 1) for k in places], axis=0
    )


def kernel(sizes, pops_ref, temp_ref, diff_ref, nozzle_ref, wall_ref, load_ref, cool_ref,
           out_ref, solid_ref, pops, post, temp, diff, first, links, base, inverse, heat,
           sx_in, sy_out, sy_in, heat_out, heat_in, px_in, py_out, py_in, pz_out, pz_in,
           xy_in, xz_out, xz_in, yz_out, yz_in, fx_in, fy_out, fy_in,
           load_sem, send_sem, recv_sem):
    nx, ny, nz = sizes
    gx, gy, gz = (lax.axis_index(name) for name in ("gx", "gy", "gz"))
    X, Z, Y = pops.shape[1:]
    D, W = temp.shape[1:]
    lowest = gz == 0

    def device(dx, dy, other):
        return (lax.rem(gx + dx + nx, nx), lax.rem(gy + dy + ny, ny), 1 - gz if other else gz)

    ahead = (gx, lax.rem(gy + gz, ny), 1 - gz)
    behind = (gx, lax.rem(gy + gz - 1 + ny, ny), 1 - gz)

    near = set()
    for dx, dy, other in (
        [(s, 0, 0) for s in (1, -1)] + [(0, s, 0) for s in (1, -1)] + [(0, 0, 1)]
        + [(s, t, 0) for s in (1, -1) for t in (1, -1)]
        + [(s, 0, 1) for s in (1, -1)] + [(0, s, 1) for s in (1, -1)]
    ):
        near.add((dx % nx, dy % ny, other))
    barrier = pltpu.get_barrier_semaphore()
    for dx, dy, other in sorted(near):
        pl.semaphore_signal(
            barrier, inc=1, device_id=device(dx, dy, other), device_id_type=MESH
        )

    loads = [
        pltpu.make_async_copy(temp_ref, temp, load_sem.at[X]),
        pltpu.make_async_copy(diff_ref, diff, load_sem.at[X + 1]),
    ]
    for copy in loads:
        copy.start()
    turn = [X - 1] + list(range(X - 1))
    for x in turn:
        pltpu.make_async_copy(pops_ref.at[:, x], pops.at[:, x], load_sem.at[x]).start()

    sent = []

    def send(source, target, where):
        place = len(sent)
        copy = pltpu.make_async_remote_copy(
            src_ref=source, dst_ref=target, send_sem=send_sem.at[place],
            recv_sem=recv_sem.at[place], device_id=where, device_id_type=MESH,
        )
        copy.start()
        sent.append(copy)
        return copy

    def blocks(ref):
        return [ref[x, z:z + ROWS, :] for x in range(X) for z in range(0, D, ROWS)]

    depth_blocks = D // ROWS
    for copy in loads:
        copy.wait()
    halved = [0.5 * tile for tile in blocks(diff)]
    sy_out[0] = edge_pack(blocks(temp) + halved, True)
    sy_out[1] = edge_pack(blocks(temp) + halved, False)
    pl.semaphore_wait(barrier, len(near))
    sink_in = []
    for side, (edge, dx) in enumerate(((X - 1, 1), (0, -1))):
        sink_in.append(send(temp.at[edge], sx_in.at[side, 0], device(dx, 0, 0)))
        sink_in.append(send(diff.at[edge], sx_in.at[side, 1], device(dx, 0, 0)))
    sink_in.append(send(sy_out.at[0], sy_in.at[0], ahead))
    sink_in.append(send(sy_out.at[1], sy_in.at[1], behind))

    def collide_plane(step, carry):
        x = lax.rem(step + X - 1, X)
        pltpu.make_async_copy(pops_ref.at[:, x], pops.at[:, x], load_sem.at[x]).wait()
        for z in range(0, Z, ROWS):
            for y in range(0, Y, LANES):
                tile = [pops[i, x, z:z + ROWS, y:y + LANES] for i in range(COUNT)]
                done, square = collide(tile)
                for i in range(COUNT):
                    post[SLOT[i], x, z:z + ROWS, y:y + LANES] = done[i]
                if z == 0:
                    heat[x, :, y:y + LANES] = H_BASE + H_GAIN * square
        return carry

    lax.fori_loop(0, 2, collide_plane, 0)
    face_in, edge_in = [], []
    for side, (edge, dx) in enumerate(((X - 1, 1), (0, -1))):
        face_in.append(
            send(post.at[pl.ds(side * FACE, FACE), edge], px_in.at[side], device(dx, 0, 0))
        )
    for side, (edge, dx) in enumerate(((X - 1, 1), (0, -1))):
        for flank, (lane, dy) in enumerate(((Y - LANES, 1), (0, -1))):
            member = SLOT[INDEX[(dx, dy, 0)]]
            edge_in.append(send(
                post.at[member, edge, :, pl.ds(lane, LANES)], xy_in.at[side, flank],
                device(dx, dy, 0),
            ))
    lax.fori_loop(2, X, collide_plane, 0)

    for x in range(X):
        heat_out[x:x + 1, :] = heat[x, 0:1, W:2 * W]
    heat_copy = send(heat_out, heat_in, device(0, 0, 1))

    for side, (lane, dy) in enumerate(((Y - LANES, 1), (0, -1))):
        tiles = [
            post[SLOT[INDEX[(a, dy, c)]], x, z:z + ROWS, lane:lane + LANES]
            for a, c in ACROSS for x in range(X) for z in range(0, Z, ROWS)
        ]
        py_out[side] = edge_pack(tiles, dy == 1)
        edge_in.append(send(py_out.at[side], py_in.at[side], device(0, dy, 0)))
    for k, (a, b) in enumerate(ACROSS):
        for x in range(X):
            row = jnp.where(
                lowest,
                post[SLOT[INDEX[(a, b, 1)]], x, Z - 1:Z, :],
                post[SLOT[INDEX[(a, b, -1)]], x, 0:1, :],
            )
            pz_out[k * X + x:k * X + x + 1, :] = row
            if (a, x) in ((1, X - 1), (-1, 0)):
                xz_out[0 if a == 1 else 1, 0:1, :] = row
            if b == 1:
                yz_out[0, x:x + 1, :] = row[:, Y - LANES:]
            if b == -1:
                yz_out[1, x:x + 1, :] = row[:, :LANES]
    edge_in.append(send(pz_out, pz_in, device(0, 0, 1)))
    for side, s in enumerate((1, -1)):
        edge_in.append(send(xz_out.at[side], xz_in.at[side], device(s, 0, 1)))
        edge_in.append(send(yz_out.at[side], yz_in.at[side], device(0, s, 1)))

    lane = lanes_like((D, W))
    depth = rows_like((D, W))
    column = depth_blocks * X

    def beside(value, packs, x, start):
        places = range(start + x * depth_blocks, start + (x + 1) * depth_blocks)
        low = jnp.where(lane == 0, edge_column(packs[0], places, False), turned(value, 1, 1))
        high = jnp.where(
            lane == W - 1, edge_column(packs[1], places, True), turned(value, -1, 1)
        )
        return low, high

    for copy in sink_in:
        copy.wait_recv()
    heat_copy.wait_recv()
    packs = (sy_in[0], sy_in[1])
    for x in range(X):
        own, cond = temp[x], 0.5 * diff[x]
        below = (temp[x - 1], diff[x - 1]) if x > 0 else (sx_in[0, 0], sx_in[0, 1])
        above = (temp[x + 1], diff[x + 1]) if x < X - 1 else (sx_in[1, 0], sx_in[1, 1])
        temps = [below[0], above[0], *beside(own, packs, x, 0)]
        conds = [0.5 * below[1], 0.5 * above[1], *beside(cond, packs, x, column)]
        g = [cond + c for c in conds]
        g.append(jnp.where(depth == D - 1, 0.0, cond + turned(cond, -1, 0)))
        g.append(jnp.where(depth == 0, 0.0, cond + turned(cond, 1, 0)))
        temps += [turned(own, -1, 0), turned(own, 1, 0)]
        warm = jnp.where(lowest, heat[x, 0:1, 0:W], heat_in[x:x + 1, :])
        start = own + jnp.where(depth == 0, load_ref[x:x + 1, :], 0.0)
        start = start + jnp.where(depth == D - 1, warm * cool_ref[x:x + 1, :], 0.0)
        denom = 1.0 + jnp.where(depth == D - 1, warm, 0.0)
        numer = start
        for k in range(6):
            numer = numer + g[k] * temps[k]
            denom = denom + g[k]
            links[k, x] = g[k]
        flip = 1.0 / denom
        base[x] = start
        inverse[x] = flip
        first[x] = numer * flip
    first_in = []
    for side, (edge, dx) in enumerate(((X - 1, 1), (0, -1))):
        first_in.append(send(first.at[edge], fx_in.at[side], device(dx, 0, 0)))
    fy_out[0] = edge_pack(blocks(first), True)
    first_in.append(send(fy_out.at[0], fy_in.at[0], ahead))
    fy_out[1] = edge_pack(blocks(first), False)
    first_in.append(send(fy_out.at[1], fy_in.at[1], behind))

    wide = lanes_like((Z, Y))
    flat = lanes_like((1, Y))
    level = rows_like((Z, Y))

    def shifted(value, lanes, border, b):
        parts = [border, value[:, LANES:]] if b == 1 else [value[:, :Y - LANES], border]
        edge = jnp.concatenate(parts, axis=1)
        spot = 0 if b == 1 else Y - 1
        return jnp.where(lanes == spot, edge, turned(value, b, 1))

    for copy in edge_in:
        copy.wait_recv()
    tall = Z // ROWS
    py_packs = (py_in[0], py_in[1])

    def assemble(x):
        height_rows = {}
        for k, (a, b) in enumerate(ACROSS):
            source = x - a
            if 0 <= source < X:
                row = pz_in[k * X + source:k * X + source + 1, :]
            else:
                row = xz_in[0 if a == 1 else 1, 0:1, :]
            if b != 0:
                flank = 0 if b == 1 else 1
                border = turned(yz_in[flank], b, 1)[x:x + 1, :]
                row = shifted(row, flat, border, b)
            height_rows[(a, b)] = row
        nozzle = nozzle_ref[x:x + 1, :] == 1
        outlet = wall_ref[x:x + 1, :] == 1
        for i, (a, b, c) in enumerate(VELOCITIES):
            source = x - a
            side = 0 if a == 1 else 1
            inside = 0 <= source < X
            value = post[SLOT[i], source] if inside else px_in[side, SLOT[i] - side * FACE]
            if b != 0:
                flank = 0 if b == 1 else 1
                if inside:
                    begin = (ACROSS.index((a, c)) * X + source) * tall
                    border = edge_column(
                        py_packs[flank], range(begin, begin + tall), b == -1
                    )
                else:
                    border = turned(xy_in[side, flank], b, 1)
                value = shifted(value, wide, border, b)
            if c != 0:
                value = turned(value, c, 0)
                back = SLOT[OPPOSITE[i]]
                if c == 1:
                    row = jnp.where(lowest, post[back, x, 0:1, :], height_rows[(a, b)])
                    value = jnp.where(level == 0, row, value)
                else:
                    closed = post[back, x, Z - 1:Z, :]
                    jet = closed + 6.0 * WEIGHTS[i] * JET_SPEED
                    plate = jnp.where(
                        nozzle, jet, jnp.where(outlet, post[SLOT[i], x, Z - 1:Z, :], closed)
                    )
                    row = jnp.where(lowest, height_rows[(a, b)], plate)
                    value = jnp.where(level == Z - 1, row, value)
            out_ref[i, x] = value

    for x in range(1, X - 1):
        assemble(x)
    for copy in face_in:
        copy.wait_recv()
    assemble(0)
    assemble(X - 1)

    for copy in first_in:
        copy.wait_recv()
    packs = (fy_in[0], fy_in[1])
    for x in range(X):
        own = first[x]
        below = first[x - 1] if x > 0 else fx_in[0]
        above = first[x + 1] if x < X - 1 else fx_in[1]
        temps = [below, above, *beside(own, packs, x, 0), turned(own, -1, 0), turned(own, 1, 0)]
        numer = base[x]
        for k in range(6):
            numer = numer + links[k, x] * temps[k]
        solid_ref[x] = numer * inverse[x]
    for copy in sent:
        copy.wait_send()


def body(populations, nozzle_mask, wall_type, solid_temp, diffusion, heat_load, coolant_temp):
    sizes = tuple(lax.axis_size(name) for name in ("gx", "gy", "gz"))
    assert sizes[0] > 1 and sizes[1] > 1 and sizes[2] == 2
    _, X, Z, Y = populations.shape
    _, D, W = solid_temp.shape
    assert X >= 2 and W == LANES and Y == sizes[2] * W and Z % ROWS == 0 and D % ROWS == 0
    assert 2 * X * (D // ROWS) <= LANES and len(ACROSS) * X * (Z // ROWS) <= LANES
    rows = -(-len(ACROSS) * X // ROWS) * ROWS
    tall = -(-X // ROWS) * ROWS

    def vmem(*shape):
        return pltpu.VMEM(shape, jnp.float32)

    pair = vmem(2, ROWS, LANES)
    scratch = [
        vmem(COUNT, X, Z, Y), vmem(COUNT, X, Z, Y),
        vmem(X, D, W), vmem(X, D, W), vmem(X, D, W),
        vmem(6, X, D, W), vmem(X, D, W), vmem(X, D, W),
        vmem(X, ROWS, Y),
        vmem(2, 2, D, W), pair, pair,
        vmem(tall, W), vmem(tall, W),
        vmem(2, FACE, Z, Y), pair, pair,
        vmem(rows, Y), vmem(rows, Y),
        vmem(2, 2, Z, LANES), vmem(2, ROWS, Y), vmem(2, ROWS, Y),
        vmem(2, tall, LANES), vmem(2, tall, LANES),
        vmem(2, D, W), pair, pair,
        pltpu.SemaphoreType.DMA((X + 2,)),
        pltpu.SemaphoreType.DMA((24,)),
        pltpu.SemaphoreType.DMA((24,)),
    ]
    anywhere = pl.BlockSpec(memory_space=pl.ANY)
    local = pl.BlockSpec(memory_space=pltpu.VMEM)
    return pl.pallas_call(
        functools.partial(kernel, sizes),
        out_shape=OUTS(populations, solid_temp),
        in_specs=[anywhere] * 3 + [local] * 4,
        out_specs=[local, local],
        scratch_shapes=scratch,
        compiler_params=pltpu.CompilerParams(
            collective_id=0, has_side_effects=True, vmem_limit_bytes=24 * 1024 * 1024
        ),
    )(populations, solid_temp, diffusion, nozzle_mask, wall_type, heat_load, coolant_temp)


def OUTS(populations, solid_temp):
    return (
        pltpu.VMEM(populations.shape, jnp.float32),
        pltpu.VMEM(solid_temp.shape, jnp.float32),
    )


def solution(mesh):
    placed = (
        P(None, "gx", "gz", "gy"),
        P("gx", "gy"),
        P("gx", "gy"),
        P("gx", None, ("gy", "gz")),
        P("gx", None, ("gy", "gz")),
        P("gx", ("gy", "gz")),
        P("gx", ("gy", "gz")),
    )
    return jax.shard_map(
        body,
        mesh=mesh,
        in_specs=placed,
        out_specs=(P(None, "gx", "gz", "gy"), P("gx", None, ("gy", "gz"))),
        check_vma=False,
    )
```

```python
import functools
import jax
import jax.numpy as jnp
import numpy as np
from jax import lax
from jax.experimental import pallas as pl
from jax.experimental.pallas import tpu as pltpu
from jax.sharding import PartitionSpec as P

JET_SPEED = 0.1
H_BASE = 0.5
H_GAIN = 40.0
LANES = 128
ROWS = 8
MESH = pl.DeviceIdType.MESH

VELOCITIES = [
    (0, 0, 0),
    (1, 0, 0), (-1, 0, 0), (0, 1, 0), (0, -1, 0), (0, 0, 1), (0, 0, -1),
    (1, 1, 0), (-1, -1, 0), (1, -1, 0), (-1, 1, 0),
    (1, 0, 1), (-1, 0, -1), (1, 0, -1), (-1, 0, 1),
    (0, 1, 1), (0, -1, -1), (0, 1, -1), (0, -1, 1),
]
COUNT = len(VELOCITIES)
WEIGHTS = [1.0 / 3.0] + [1.0 / 18.0] * 6 + [1.0 / 36.0] * 12
INDEX = {velocity: member for member, velocity in enumerate(VELOCITIES)}
OPPOSITE = [INDEX[(-a, -b, -c)] for a, b, c in VELOCITIES]
ORDER = [i for s in (1, -1, 0) for i in range(COUNT) if VELOCITIES[i][0] == s]
SLOT = {member: place for place, member in enumerate(ORDER)}
FACE = sum(1 for v in VELOCITIES if v[0] == 1)
ACROSS = [(0, 0), (1, 0), (-1, 0), (0, 1), (0, -1)]


def collide(f):
    s = {i: f[i] + f[i + 1] for i in range(1, COUNT, 2)}
    d = {i: f[i] - f[i + 1] for i in range(1, COUNT, 2)}
    jx = (d[1] + d[7]) + (d[9] + d[11]) + d[13]
    jy = (d[3] + d[7]) + (d[15] - d[9]) + d[17]
    jz = (d[5] + d[11]) + (d[15] - d[13]) - d[17]
    sxy, sxz, syz = s[7] + s[9], s[11] + s[13], s[15] + s[17]
    rho = f[0] + (s[1] + s[3] + s[5]) + (sxy + sxz + syz)
    inv = 1.0 / rho
    ux, uy, uz = jx * inv, jy * inv, jz * inv
    px, py, pz = jx * ux, jy * uy, jz * uz
    p = px + py + pz
    base = rho - 1.5 * p
    hxy, hxz, hyz = px + py, px + pz, py + pz
    c4 = 4.0 * f[0] - base
    qxy = c4 + sxy - 2.0 * (s[1] + s[3]) + 0.5 * hxy
    qxz = c4 + sxz - 2.0 * (s[1] + s[5]) + 0.5 * hxz
    qyz = c4 + syz - 2.0 * (s[3] + s[5]) + 0.5 * hyz
    mean = (qxy + qxz + qyz) * (2.0 / 7.0)
    txy, txz, tyz = ((q - mean) * (0.2 / 12.0) for q in (qxy, qxz, qyz))
    post = [None] * COUNT
    post[0] = (1.6 / 3.0) * base - 0.6 * f[0] + 4.0 * (txy + txz + tyz)
    axis_base = (1.6 / 18.0) * base
    for i, pp, tt, j in ((1, px, txy + txz, jx), (3, py, txy + tyz, jy), (5, pz, txz + tyz, jz)):
        even = axis_base + 0.4 * pp - 0.3 * s[i] - 2.0 * tt
        odd = 0.2 * j - 0.1 * d[i]
        post[i], post[i + 1] = even + odd, even - odd
    diag_base = (1.6 / 36.0) * base
    for i, hh, tt, j, k, u in (
        (7, hxy, txy, jx, jy, uy), (11, hxz, txz, jx, jz, uz), (15, hyz, tyz, jy, jz, uz)
    ):
        both = diag_base + 0.2 * hh + tt
        cross = 0.4 * (j * u)
        even = both + cross - 0.3 * s[i]
        odd = 0.1 * (j + k - d[i])
        post[i], post[i + 1] = even + odd, even - odd
        even = both - cross - 0.3 * s[i + 2]
        odd = 0.1 * (j - k - d[i + 2])
        post[i + 2], post[i + 3] = even + odd, even - odd
    return post, p * inv


def lanes_like(shape):
    return lax.broadcasted_iota(jnp.int32, shape, len(shape) - 1)


def rows_like(shape):
    return lax.broadcasted_iota(jnp.int32, shape, len(shape) - 2)


def turned(value, shift, axis):
    shift = shift % value.shape[axis]
    return value if shift == 0 else pltpu.roll(value, shift, axis)


def edge_pack(tiles, last):
    lane = lanes_like((ROWS, LANES))
    packed = jnp.zeros((ROWS, LANES), jnp.float32)
    for k, tile in enumerate(tiles):
        packed = jnp.where(lane == k, turned(tile, k + 1 if last else k, 1), packed)
    return packed


def edge_column(packed, places, last):
    return jnp.concatenate(
        [turned(packed, (LANES - 1 if last else 0) - k, 1) for k in places], axis=0
    )


def kernel(sizes, pops_ref, temp_ref, diff_ref, nozzle_hbm, wall_hbm, load_hbm, cool_hbm,
           out_ref, solid_ref, nozzle_ref, wall_ref, load_ref, cool_ref, pops, post, temp, diff, first, links, base, inverse, heat,
           sx_in, sy_out, sy_in, heat_out, heat_in, px_in, py_out, py_in, pz_out, pz_in,
           xy_in, xz_out, xz_in, yz_out, yz_in, fx_in, fy_out, fy_in,
           load_sem, send_sem, recv_sem):
    nx, ny, nz = sizes
    gx, gy, gz = (lax.axis_index(name) for name in ("gx", "gy", "gz"))
    X, Z, Y = pops.shape[1:]
    D, W = temp.shape[1:]
    lowest = gz == 0

    def device(dx, dy, other):
        return (lax.rem(gx + dx + nx, nx), lax.rem(gy + dy + ny, ny), 1 - gz if other else gz)

    ahead = (gx, lax.rem(gy + gz, ny), 1 - gz)
    behind = (gx, lax.rem(gy + gz - 1 + ny, ny), 1 - gz)

    near = set()
    for dx, dy, other in (
        [(s, 0, 0) for s in (1, -1)] + [(0, s, 0) for s in (1, -1)] + [(0, 0, 1)]
        + [(s, t, 0) for s in (1, -1) for t in (1, -1)]
        + [(s, 0, 1) for s in (1, -1)] + [(0, s, 1) for s in (1, -1)]
    ):
        near.add((dx % nx, dy % ny, other))
    barrier = pltpu.get_barrier_semaphore()
    for dx, dy, other in sorted(near):
        pl.semaphore_signal(
            barrier, inc=1, device_id=device(dx, dy, other), device_id_type=MESH
        )

    loads = [
        pltpu.make_async_copy(temp_ref, temp, load_sem.at[X]),
        pltpu.make_async_copy(diff_ref, diff, load_sem.at[X + 1]),
    ]
    planes = [
        pltpu.make_async_copy(far, near_by, load_sem.at[X + 2 + k])
        for k, (far, near_by) in enumerate((
            (nozzle_hbm, nozzle_ref), (wall_hbm, wall_ref),
            (load_hbm, load_ref), (cool_hbm, cool_ref),
        ))
    ]
    for copy in loads:
        copy.start()
    turn = [X - 1] + list(range(X - 1))
    for x in turn:
        pltpu.make_async_copy(pops_ref.at[:, x], pops.at[:, x], load_sem.at[x]).start()
    for copy in planes:
        copy.start()

    sent = []

    def send(source, target, where):
        place = len(sent)
        copy = pltpu.make_async_remote_copy(
            src_ref=source, dst_ref=target, send_sem=send_sem.at[place],
            recv_sem=recv_sem.at[place], device_id=where, device_id_type=MESH,
        )
        copy.start()
        sent.append(copy)
        return copy

    def blocks(ref):
        return [ref[x, z:z + ROWS, :] for x in range(X) for z in range(0, D, ROWS)]

    pl.semaphore_wait(barrier, len(near))
    sink_in = []
    for side, (edge, dx) in enumerate(((X - 1, 1), (0, -1))):
        sink_in.append(send(temp_ref.at[edge], sx_in.at[side, 0], device(dx, 0, 0)))
        sink_in.append(send(diff_ref.at[edge], sx_in.at[side, 1], device(dx, 0, 0)))

    def collide_plane(step, carry):
        x = lax.rem(step + X - 1, X)
        pltpu.make_async_copy(pops_ref.at[:, x], pops.at[:, x], load_sem.at[x]).wait()
        for z in range(0, Z, ROWS):
            for y in range(0, Y, LANES):
                tile = [pops[i, x, z:z + ROWS, y:y + LANES] for i in range(COUNT)]
                done, square = collide(tile)
                for i in range(COUNT):
                    post[SLOT[i], x, z:z + ROWS, y:y + LANES] = done[i]
                if z == 0:
                    heat[x, :, y:y + LANES] = H_BASE + H_GAIN * square
        return carry

    lax.fori_loop(0, 2, collide_plane, 0)
    face_in, edge_in = [], []
    for side, (edge, dx) in enumerate(((X - 1, 1), (0, -1))):
        face_in.append(
            send(post.at[pl.ds(side * FACE, FACE), edge], px_in.at[side], device(dx, 0, 0))
        )
    for side, (edge, dx) in enumerate(((X - 1, 1), (0, -1))):
        for flank, (lane, dy) in enumerate(((Y - LANES, 1), (0, -1))):
            member = SLOT[INDEX[(dx, dy, 0)]]
            edge_in.append(send(
                post.at[member, edge, :, pl.ds(lane, LANES)], xy_in.at[side, flank],
                device(dx, dy, 0),
            ))
    lax.fori_loop(2, X, collide_plane, 0)

    for copy in loads:
        copy.wait()
    halved = [0.5 * tile for tile in blocks(diff)]
    sy_out[0] = edge_pack(blocks(temp) + halved, True)
    sink_in.append(send(sy_out.at[0], sy_in.at[0], ahead))
    sy_out[1] = edge_pack(blocks(temp) + halved, False)
    sink_in.append(send(sy_out.at[1], sy_in.at[1], behind))

    for x in range(X):
        heat_out[x:x + 1, :] = heat[x, 0:1, W:2 * W]
    heat_copy = send(heat_out, heat_in, device(0, 0, 1))

    for side, (lane, dy) in enumerate(((Y - LANES, 1), (0, -1))):
        tiles = [
            post[SLOT[INDEX[(a, dy, c)]], x, z:z + ROWS, lane:lane + LANES]
            for a, c in ACROSS for x in range(X) for z in range(0, Z, ROWS)
        ]
        py_out[side] = edge_pack(tiles, dy == 1)
        edge_in.append(send(py_out.at[side], py_in.at[side], device(0, dy, 0)))
    for k, (a, b) in enumerate(ACROSS):
        for x in range(X):
            row = jnp.where(
                lowest,
                post[SLOT[INDEX[(a, b, 1)]], x, Z - 1:Z, :],
                post[SLOT[INDEX[(a, b, -1)]], x, 0:1, :],
            )
            pz_out[k * X + x:k * X + x + 1, :] = row
            if (a, x) in ((1, X - 1), (-1, 0)):
                xz_out[0 if a == 1 else 1, 0:1, :] = row
            if b == 1:
                yz_out[0, x:x + 1, :] = row[:, Y - LANES:]
            if b == -1:
                yz_out[1, x:x + 1, :] = row[:, :LANES]
    edge_in.append(send(pz_out, pz_in, device(0, 0, 1)))
    for side, s in enumerate((1, -1)):
        edge_in.append(send(xz_out.at[side], xz_in.at[side], device(s, 0, 1)))
        edge_in.append(send(yz_out.at[side], yz_in.at[side], device(0, s, 1)))

    lane = lanes_like((D, W))
    depth = rows_like((D, W))
    depth_blocks = D // ROWS
    column = depth_blocks * X

    def beside(value, packs, x, start):
        places = range(start + x * depth_blocks, start + (x + 1) * depth_blocks)
        low = jnp.where(lane == 0, edge_column(packs[0], places, False), turned(value, 1, 1))
        high = jnp.where(
            lane == W - 1, edge_column(packs[1], places, True), turned(value, -1, 1)
        )
        return low, high

    for copy in sink_in:
        copy.wait_recv()
    heat_copy.wait_recv()
    for copy in planes:
        copy.wait()
    packs = (sy_in[0], sy_in[1])
    for x in range(X):
        own, cond = temp[x], 0.5 * diff[x]
        below = (temp[x - 1], diff[x - 1]) if x > 0 else (sx_in[0, 0], sx_in[0, 1])
        above = (temp[x + 1], diff[x + 1]) if x < X - 1 else (sx_in[1, 0], sx_in[1, 1])
        temps = [below[0], above[0], *beside(own, packs, x, 0)]
        conds = [0.5 * below[1], 0.5 * above[1], *beside(cond, packs, x, column)]
        g = [cond + c for c in conds]
        g.append(jnp.where(depth == D - 1, 0.0, cond + turned(cond, -1, 0)))
        g.append(jnp.where(depth == 0, 0.0, cond + turned(cond, 1, 0)))
        temps += [turned(own, -1, 0), turned(own, 1, 0)]
        warm = jnp.where(lowest, heat[x, 0:1, 0:W], heat_in[x:x + 1, :])
        start = own + jnp.where(depth == 0, load_ref[x:x + 1, :], 0.0)
        start = start + jnp.where(depth == D - 1, warm * cool_ref[x:x + 1, :], 0.0)
        denom = 1.0 + jnp.where(depth == D - 1, warm, 0.0)
        numer = start
        for k in range(6):
            numer = numer + g[k] * temps[k]
            denom = denom + g[k]
            links[k, x] = g[k]
        flip = 1.0 / denom
        base[x] = start
        inverse[x] = flip
        first[x] = numer * flip
    first_in = []
    for side, (edge, dx) in enumerate(((X - 1, 1), (0, -1))):
        first_in.append(send(first.at[edge], fx_in.at[side], device(dx, 0, 0)))
    fy_out[0] = edge_pack(blocks(first), True)
    first_in.append(send(fy_out.at[0], fy_in.at[0], ahead))
    fy_out[1] = edge_pack(blocks(first), False)
    first_in.append(send(fy_out.at[1], fy_in.at[1], behind))

    wide = lanes_like((Z, Y))
    flat = lanes_like((1, Y))
    level = rows_like((Z, Y))

    def shifted(value, lanes, border, b):
        parts = [border, value[:, LANES:]] if b == 1 else [value[:, :Y - LANES], border]
        edge = jnp.concatenate(parts, axis=1)
        spot = 0 if b == 1 else Y - 1
        return jnp.where(lanes == spot, edge, turned(value, b, 1))

    for copy in edge_in:
        copy.wait_recv()
    tall = Z // ROWS
    py_packs = (py_in[0], py_in[1])

    def assemble(x):
        height_rows = {}
        for k, (a, b) in enumerate(ACROSS):
            source = x - a
            if 0 <= source < X:
                row = pz_in[k * X + source:k * X + source + 1, :]
            else:
                row = xz_in[0 if a == 1 else 1, 0:1, :]
            if b != 0:
                flank = 0 if b == 1 else 1
                border = turned(yz_in[flank], b, 1)[x:x + 1, :]
                row = shifted(row, flat, border, b)
            height_rows[(a, b)] = row
        nozzle = nozzle_ref[x:x + 1, :] == 1
        outlet = wall_ref[x:x + 1, :] == 1
        for i, (a, b, c) in enumerate(VELOCITIES):
            source = x - a
            side = 0 if a == 1 else 1
            inside = 0 <= source < X
            value = post[SLOT[i], source] if inside else px_in[side, SLOT[i] - side * FACE]
            if b != 0:
                flank = 0 if b == 1 else 1
                if inside:
                    begin = (ACROSS.index((a, c)) * X + source) * tall
                    border = edge_column(
                        py_packs[flank], range(begin, begin + tall), b == -1
                    )
                else:
                    border = turned(xy_in[side, flank], b, 1)
                value = shifted(value, wide, border, b)
            if c != 0:
                value = turned(value, c, 0)
                back = SLOT[OPPOSITE[i]]
                if c == 1:
                    row = jnp.where(lowest, post[back, x, 0:1, :], height_rows[(a, b)])
                    value = jnp.where(level == 0, row, value)
                else:
                    closed = post[back, x, Z - 1:Z, :]
                    jet = closed + 6.0 * WEIGHTS[i] * JET_SPEED
                    plate = jnp.where(
                        nozzle, jet, jnp.where(outlet, post[SLOT[i], x, Z - 1:Z, :], closed)
                    )
                    row = jnp.where(lowest, height_rows[(a, b)], plate)
                    value = jnp.where(level == Z - 1, row, value)
            out_ref[i, x] = value

    for x in range(1, X - 1):
        assemble(x)
    for copy in face_in:
        copy.wait_recv()
    assemble(0)
    assemble(X - 1)

    for copy in first_in:
        copy.wait_recv()
    packs = (fy_in[0], fy_in[1])
    for x in range(X):
        own = first[x]
        below = first[x - 1] if x > 0 else fx_in[0]
        above = first[x + 1] if x < X - 1 else fx_in[1]
        temps = [below, above, *beside(own, packs, x, 0), turned(own, -1, 0), turned(own, 1, 0)]
        numer = base[x]
        for k in range(6):
            numer = numer + links[k, x] * temps[k]
        solid_ref[x] = numer * inverse[x]
    for copy in sent:
        copy.wait_send()


def body(populations, nozzle_mask, wall_type, solid_temp, diffusion, heat_load, coolant_temp):
    sizes = tuple(lax.axis_size(name) for name in ("gx", "gy", "gz"))
    assert sizes[0] > 1 and sizes[1] > 1 and sizes[2] == 2
    _, X, Z, Y = populations.shape
    _, D, W = solid_temp.shape
    assert X >= 2 and W == LANES and Y == sizes[2] * W and Z % ROWS == 0 and D % ROWS == 0
    assert 2 * X * (D // ROWS) <= LANES and len(ACROSS) * X * (Z // ROWS) <= LANES
    rows = -(-len(ACROSS) * X // ROWS) * ROWS
    tall = -(-X // ROWS) * ROWS

    def vmem(*shape):
        return pltpu.VMEM(shape, jnp.float32)

    pair = vmem(2, ROWS, LANES)
    scratch = [
        pltpu.VMEM((X, Y), jnp.int32), pltpu.VMEM((X, Y), jnp.int32), vmem(X, W), vmem(X, W),
        vmem(COUNT, X, Z, Y), vmem(COUNT, X, Z, Y),
        vmem(X, D, W), vmem(X, D, W), vmem(X, D, W),
        vmem(6, X, D, W), vmem(X, D, W), vmem(X, D, W),
        vmem(X, ROWS, Y),
        vmem(2, 2, D, W), pair, pair,
        vmem(tall, W), vmem(tall, W),
        vmem(2, FACE, Z, Y), pair, pair,
        vmem(rows, Y), vmem(rows, Y),
        vmem(2, 2, Z, LANES), vmem(2, ROWS, Y), vmem(2, ROWS, Y),
        vmem(2, tall, LANES), vmem(2, tall, LANES),
        vmem(2, D, W), pair, pair,
        pltpu.SemaphoreType.DMA((X + 6,)),
        pltpu.SemaphoreType.DMA((24,)),
        pltpu.SemaphoreType.DMA((24,)),
    ]
    far = pl.BlockSpec(memory_space=pltpu.HBM)
    local = pl.BlockSpec(memory_space=pltpu.VMEM)
    moved, swept = pl.pallas_call(
        functools.partial(kernel, sizes),
        out_shape=(
            pltpu.VMEM(populations.shape, jnp.float32),
            pltpu.VMEM(solid_temp.shape, jnp.float32),
        ),
        in_specs=[far] * 7,
        out_specs=[local, local],
        scratch_shapes=scratch,
        compiler_params=pltpu.CompilerParams(
            collective_id=0, has_side_effects=True, vmem_limit_bytes=24 * 1024 * 1024
        ),
    )(*(
        pltpu.with_memory_space_constraint(value, pltpu.HBM)
        for value in (populations, solid_temp, diffusion, nozzle_mask, wall_type, heat_load,
                      coolant_temp)
    ))
    return pl.pallas_call(
        deliver,
        out_shape=(
            pltpu.HBM(populations.shape, jnp.float32),
            pltpu.HBM(solid_temp.shape, jnp.float32),
        ),
        in_specs=[local, local],
        out_specs=[far, far],
        scratch_shapes=[pltpu.SemaphoreType.DMA((2,))],
    )(moved, swept)


def deliver(moved_ref, swept_ref, out_ref, solid_ref, sem):
    copies = [
        pltpu.make_async_copy(moved_ref, out_ref, sem.at[0]),
        pltpu.make_async_copy(swept_ref, solid_ref, sem.at[1]),
    ]
    for copy in copies:
        copy.start()
    for copy in copies:
        copy.wait()


def solution(mesh):
    placed = (
        P(None, "gx", "gz", "gy"),
        P("gx", "gy"),
        P("gx", "gy"),
        P("gx", None, ("gy", "gz")),
        P("gx", None, ("gy", "gz")),
        P("gx", ("gy", "gz")),
        P("gx", ("gy", "gz")),
    )
    return jax.shard_map(
        body,
        mesh=mesh,
        in_specs=placed,
        out_specs=(P(None, "gx", "gz", "gy"), P("gx", None, ("gy", "gz"))),
        check_vma=False,
    )
```

```python
import functools
import jax
import jax.numpy as jnp
import numpy as np
from jax import lax
from jax.experimental import pallas as pl
from jax.experimental.pallas import tpu as pltpu
from jax.sharding import PartitionSpec as P

JET_SPEED = 0.1
H_BASE = 0.5
H_GAIN = 40.0
LANES = 128
ROWS = 8
MESH = pl.DeviceIdType.MESH

VELOCITIES = [
    (0, 0, 0),
    (1, 0, 0), (-1, 0, 0), (0, 1, 0), (0, -1, 0), (0, 0, 1), (0, 0, -1),
    (1, 1, 0), (-1, -1, 0), (1, -1, 0), (-1, 1, 0),
    (1, 0, 1), (-1, 0, -1), (1, 0, -1), (-1, 0, 1),
    (0, 1, 1), (0, -1, -1), (0, 1, -1), (0, -1, 1),
]
COUNT = len(VELOCITIES)
WEIGHTS = [1.0 / 3.0] + [1.0 / 18.0] * 6 + [1.0 / 36.0] * 12
INDEX = {velocity: member for member, velocity in enumerate(VELOCITIES)}
OPPOSITE = [INDEX[(-a, -b, -c)] for a, b, c in VELOCITIES]
ORDER = [i for s in (1, -1, 0) for i in range(COUNT) if VELOCITIES[i][0] == s]
SLOT = {member: place for place, member in enumerate(ORDER)}
FACE = sum(1 for v in VELOCITIES if v[0] == 1)
ACROSS = [(0, 0), (1, 0), (-1, 0), (0, 1), (0, -1)]


def collide(f):
    s = {i: f[i] + f[i + 1] for i in range(1, COUNT, 2)}
    d = {i: f[i] - f[i + 1] for i in range(1, COUNT, 2)}
    jx = (d[1] + d[7]) + (d[9] + d[11]) + d[13]
    jy = (d[3] + d[7]) + (d[15] - d[9]) + d[17]
    jz = (d[5] + d[11]) + (d[15] - d[13]) - d[17]
    sxy, sxz, syz = s[7] + s[9], s[11] + s[13], s[15] + s[17]
    rho = f[0] + (s[1] + s[3] + s[5]) + (sxy + sxz + syz)
    inv = 1.0 / rho
    ux, uy, uz = jx * inv, jy * inv, jz * inv
    px, py, pz = jx * ux, jy * uy, jz * uz
    p = px + py + pz
    base = rho - 1.5 * p
    hxy, hxz, hyz = px + py, px + pz, py + pz
    c4 = 4.0 * f[0] - base
    qxy = c4 + sxy - 2.0 * (s[1] + s[3]) + 0.5 * hxy
    qxz = c4 + sxz - 2.0 * (s[1] + s[5]) + 0.5 * hxz
    qyz = c4 + syz - 2.0 * (s[3] + s[5]) + 0.5 * hyz
    mean = (qxy + qxz + qyz) * (2.0 / 7.0)
    txy, txz, tyz = ((q - mean) * (0.2 / 12.0) for q in (qxy, qxz, qyz))
    post = [None] * COUNT
    post[0] = (1.6 / 3.0) * base - 0.6 * f[0] + 4.0 * (txy + txz + tyz)
    axis_base = (1.6 / 18.0) * base
    for i, pp, tt, j in ((1, px, txy + txz, jx), (3, py, txy + tyz, jy), (5, pz, txz + tyz, jz)):
        even = axis_base + 0.4 * pp - 0.3 * s[i] - 2.0 * tt
        odd = 0.2 * j - 0.1 * d[i]
        post[i], post[i + 1] = even + odd, even - odd
    diag_base = (1.6 / 36.0) * base
    for i, hh, tt, j, k, u in (
        (7, hxy, txy, jx, jy, uy), (11, hxz, txz, jx, jz, uz), (15, hyz, tyz, jy, jz, uz)
    ):
        both = diag_base + 0.2 * hh + tt
        cross = 0.4 * (j * u)
        even = both + cross - 0.3 * s[i]
        odd = 0.1 * (j + k - d[i])
        post[i], post[i + 1] = even + odd, even - odd
        even = both - cross - 0.3 * s[i + 2]
        odd = 0.1 * (j - k - d[i + 2])
        post[i + 2], post[i + 3] = even + odd, even - odd
    return post, p * inv


def lanes_like(shape):
    return lax.broadcasted_iota(jnp.int32, shape, len(shape) - 1)


def rows_like(shape):
    return lax.broadcasted_iota(jnp.int32, shape, len(shape) - 2)


def turned(value, shift, axis):
    shift = shift % value.shape[axis]
    return value if shift == 0 else pltpu.roll(value, shift, axis)


def edge_pack(tiles, last):
    lane = lanes_like((ROWS, LANES))
    packed = jnp.zeros((ROWS, LANES), jnp.float32)
    for k, tile in enumerate(tiles):
        packed = jnp.where(lane == k, turned(tile, k + 1 if last else k, 1), packed)
    return packed


def edge_column(packed, places, last):
    return jnp.concatenate(
        [turned(packed, (LANES - 1 if last else 0) - k, 1) for k in places], axis=0
    )


def kernel(sizes, pops_ref, temp_ref, diff_ref, nozzle_hbm, wall_hbm, load_hbm, cool_hbm,
           out_ref, solid_ref, nozzle_ref, wall_ref, load_ref, cool_ref, pops, post, temp, diff, first, links, base, inverse, heat,
           sx_in, sy_out, sy_in, heat_out, heat_in, px_in, py_out, py_in, pz_out, pz_in,
           xy_in, xz_out, xz_in, yz_out, yz_in, fx_in, fy_out, fy_in,
           load_sem, send_sem, recv_sem):
    nx, ny, nz = sizes
    gx, gy, gz = (lax.axis_index(name) for name in ("gx", "gy", "gz"))
    X, Z, Y = pops.shape[1:]
    D, W = temp.shape[1:]
    lowest = gz == 0

    def device(dx, dy, other):
        return (lax.rem(gx + dx + nx, nx), lax.rem(gy + dy + ny, ny), 1 - gz if other else gz)

    ahead = (gx, lax.rem(gy + gz, ny), 1 - gz)
    behind = (gx, lax.rem(gy + gz - 1 + ny, ny), 1 - gz)

    near = set()
    for dx, dy, other in (
        [(s, 0, 0) for s in (1, -1)] + [(0, s, 0) for s in (1, -1)] + [(0, 0, 1)]
        + [(s, t, 0) for s in (1, -1) for t in (1, -1)]
        + [(s, 0, 1) for s in (1, -1)] + [(0, s, 1) for s in (1, -1)]
    ):
        near.add((dx % nx, dy % ny, other))
    barrier = pltpu.get_barrier_semaphore()
    for dx, dy, other in sorted(near):
        pl.semaphore_signal(
            barrier, inc=1, device_id=device(dx, dy, other), device_id_type=MESH
        )

    loads = [
        pltpu.make_async_copy(temp_ref, temp, load_sem.at[X]),
        pltpu.make_async_copy(diff_ref, diff, load_sem.at[X + 1]),
    ]
    planes = [
        pltpu.make_async_copy(far, near_by, load_sem.at[X + 2 + k])
        for k, (far, near_by) in enumerate((
            (nozzle_hbm, nozzle_ref), (wall_hbm, wall_ref),
            (load_hbm, load_ref), (cool_hbm, cool_ref),
        ))
    ]
    for copy in loads:
        copy.start()
    turn = [X - 1] + list(range(X - 1))
    for x in turn:
        pltpu.make_async_copy(pops_ref.at[:, x], pops.at[:, x], load_sem.at[x]).start()
    for copy in planes:
        copy.start()

    sent = []

    def send(source, target, where):
        place = len(sent)
        copy = pltpu.make_async_remote_copy(
            src_ref=source, dst_ref=target, send_sem=send_sem.at[place],
            recv_sem=recv_sem.at[place], device_id=where, device_id_type=MESH,
        )
        copy.start()
        sent.append(copy)
        return copy

    def blocks(ref):
        return [ref[x, z:z + ROWS, :] for x in range(X) for z in range(0, D, ROWS)]

    pl.semaphore_wait(barrier, len(near))
    sink_in = []
    for side, (edge, dx) in enumerate(((X - 1, 1), (0, -1))):
        sink_in.append(send(temp_ref.at[edge], sx_in.at[side, 0], device(dx, 0, 0)))
        sink_in.append(send(diff_ref.at[edge], sx_in.at[side, 1], device(dx, 0, 0)))

    def collide_plane(step, carry):
        x = lax.rem(step + X - 1, X)
        pltpu.make_async_copy(pops_ref.at[:, x], pops.at[:, x], load_sem.at[x]).wait()
        for z in range(0, Z, ROWS):
            for y in range(0, Y, LANES):
                tile = [pops[i, x, z:z + ROWS, y:y + LANES] for i in range(COUNT)]
                done, square = collide(tile)
                for i in range(COUNT):
                    post[SLOT[i], x, z:z + ROWS, y:y + LANES] = done[i]
                if z == 0:
                    heat[x, :, y:y + LANES] = H_BASE + H_GAIN * square
        return carry

    lax.fori_loop(0, 2, collide_plane, 0)
    face_in, corner_in, edge_in = [], [], []
    for side, (edge, dx) in enumerate(((X - 1, 1), (0, -1))):
        face_in.append(
            send(post.at[pl.ds(side * FACE, FACE), edge], px_in.at[side], device(dx, 0, 0))
        )
    for side, (edge, dx) in enumerate(((X - 1, 1), (0, -1))):
        for flank, (lane, dy) in enumerate(((Y - LANES, 1), (0, -1))):
            member = SLOT[INDEX[(dx, dy, 0)]]
            corner_in.append(send(
                post.at[member, edge, :, pl.ds(lane, LANES)], xy_in.at[side, flank],
                device(dx, dy, 0),
            ))
    lax.fori_loop(2, X, collide_plane, 0)

    for copy in loads:
        copy.wait()
    halved = [0.5 * tile for tile in blocks(diff)]
    sy_out[0] = edge_pack(blocks(temp) + halved, True)
    flank_in = [send(sy_out.at[0], sy_in.at[0], ahead)]
    sy_out[1] = edge_pack(blocks(temp) + halved, False)
    flank_in.append(send(sy_out.at[1], sy_in.at[1], behind))

    for x in range(X):
        heat_out[x:x + 1, :] = heat[x, 0:1, W:2 * W]
    heat_copy = send(heat_out, heat_in, device(0, 0, 1))

    for side, (lane, dy) in enumerate(((Y - LANES, 1), (0, -1))):
        tiles = [
            post[SLOT[INDEX[(a, dy, c)]], x, z:z + ROWS, lane:lane + LANES]
            for a, c in ACROSS for x in range(X) for z in range(0, Z, ROWS)
        ]
        py_out[side] = edge_pack(tiles, dy == 1)
        edge_in.append(send(py_out.at[side], py_in.at[side], device(0, dy, 0)))
    for k, (a, b) in enumerate(ACROSS):
        for x in range(X):
            row = jnp.where(
                lowest,
                post[SLOT[INDEX[(a, b, 1)]], x, Z - 1:Z, :],
                post[SLOT[INDEX[(a, b, -1)]], x, 0:1, :],
            )
            pz_out[k * X + x:k * X + x + 1, :] = row
            if (a, x) in ((1, X - 1), (-1, 0)):
                xz_out[0 if a == 1 else 1, 0:1, :] = row
            if b == 1:
                yz_out[0, x:x + 1, :] = row[:, Y - LANES:]
            if b == -1:
                yz_out[1, x:x + 1, :] = row[:, :LANES]
    edge_in.append(send(pz_out, pz_in, device(0, 0, 1)))
    for side, s in enumerate((1, -1)):
        corner_in.append(send(xz_out.at[side], xz_in.at[side], device(s, 0, 1)))
        edge_in.append(send(yz_out.at[side], yz_in.at[side], device(0, s, 1)))

    lane = lanes_like((D, W))
    depth = rows_like((D, W))
    depth_blocks = D // ROWS
    column = depth_blocks * X

    def beside(value, packs, x, start):
        places = range(start + x * depth_blocks, start + (x + 1) * depth_blocks)
        low = jnp.where(lane == 0, edge_column(packs[0], places, False), turned(value, 1, 1))
        high = jnp.where(
            lane == W - 1, edge_column(packs[1], places, True), turned(value, -1, 1)
        )
        return low, high

    def sweep_first(x):
        own, cond = temp[x], 0.5 * diff[x]
        below = (temp[x - 1], diff[x - 1]) if x > 0 else (sx_in[0, 0], sx_in[0, 1])
        above = (temp[x + 1], diff[x + 1]) if x < X - 1 else (sx_in[1, 0], sx_in[1, 1])
        temps = [below[0], above[0], *beside(own, (sy_in[0], sy_in[1]), x, 0)]
        conds = [0.5 * below[1], 0.5 * above[1], *beside(cond, (sy_in[0], sy_in[1]), x, column)]
        g = [cond + c for c in conds]
        g.append(jnp.where(depth == D - 1, 0.0, cond + turned(cond, -1, 0)))
        g.append(jnp.where(depth == 0, 0.0, cond + turned(cond, 1, 0)))
        temps += [turned(own, -1, 0), turned(own, 1, 0)]
        warm = jnp.where(lowest, heat[x, 0:1, 0:W], heat_in[x:x + 1, :])
        start = own + jnp.where(depth == 0, load_ref[x:x + 1, :], 0.0)
        start = start + jnp.where(depth == D - 1, warm * cool_ref[x:x + 1, :], 0.0)
        denom = 1.0 + jnp.where(depth == D - 1, warm, 0.0)
        numer = start
        for k in range(6):
            numer = numer + g[k] * temps[k]
            denom = denom + g[k]
            links[k, x] = g[k]
        flip = 1.0 / denom
        base[x] = start
        inverse[x] = flip
        first[x] = numer * flip
    wide = lanes_like((Z, Y))
    flat = lanes_like((1, Y))
    level = rows_like((Z, Y))

    def shifted(value, lanes, border, b):
        parts = [border, value[:, LANES:]] if b == 1 else [value[:, :Y - LANES], border]
        edge = jnp.concatenate(parts, axis=1)
        spot = 0 if b == 1 else Y - 1
        return jnp.where(lanes == spot, edge, turned(value, b, 1))

    tall = Z // ROWS

    def assemble(x):
        height_rows = {}
        for k, (a, b) in enumerate(ACROSS):
            source = x - a
            if 0 <= source < X:
                row = pz_in[k * X + source:k * X + source + 1, :]
            else:
                row = xz_in[0 if a == 1 else 1, 0:1, :]
            if b != 0:
                flank = 0 if b == 1 else 1
                border = turned(yz_in[flank], b, 1)[x:x + 1, :]
                row = shifted(row, flat, border, b)
            height_rows[(a, b)] = row
        nozzle = nozzle_ref[x:x + 1, :] == 1
        outlet = wall_ref[x:x + 1, :] == 1
        for i, (a, b, c) in enumerate(VELOCITIES):
            source = x - a
            side = 0 if a == 1 else 1
            inside = 0 <= source < X
            value = post[SLOT[i], source] if inside else px_in[side, SLOT[i] - side * FACE]
            if b != 0:
                flank = 0 if b == 1 else 1
                if inside:
                    begin = (ACROSS.index((a, c)) * X + source) * tall
                    border = edge_column(
                        py_in[flank], range(begin, begin + tall), b == -1
                    )
                else:
                    border = turned(xy_in[side, flank], b, 1)
                value = shifted(value, wide, border, b)
            if c != 0:
                value = turned(value, c, 0)
                back = SLOT[OPPOSITE[i]]
                if c == 1:
                    row = jnp.where(lowest, post[back, x, 0:1, :], height_rows[(a, b)])
                    value = jnp.where(level == 0, row, value)
                else:
                    closed = post[back, x, Z - 1:Z, :]
                    jet = closed + 6.0 * WEIGHTS[i] * JET_SPEED
                    plate = jnp.where(
                        nozzle, jet, jnp.where(outlet, post[SLOT[i], x, Z - 1:Z, :], closed)
                    )
                    row = jnp.where(lowest, height_rows[(a, b)], plate)
                    value = jnp.where(level == Z - 1, row, value)
            out_ref[i, x] = value

    def sweep_second(x):
        own = first[x]
        below = first[x - 1] if x > 0 else fx_in[0]
        above = first[x + 1] if x < X - 1 else fx_in[1]
        sides = beside(own, (fy_in[0], fy_in[1]), x, 0)
        temps = [below, above, *sides, turned(own, -1, 0), turned(own, 1, 0)]
        numer = base[x]
        for k in range(6):
            numer = numer + links[k, x] * temps[k]
        solid_ref[x] = numer * inverse[x]

    inner = range(1, X - 1)
    for copy in edge_in:
        copy.wait_recv()
    for copy in planes:
        copy.wait()
    for x in inner:
        assemble(x)
    for copy in flank_in + [heat_copy]:
        copy.wait_recv()
    for x in inner:
        sweep_first(x)
    for copy in sink_in:
        copy.wait_recv()
    first_in = []
    for side, (edge, dx) in enumerate(((X - 1, 1), (0, -1))):
        sweep_first(edge)
        first_in.append(send(first.at[edge], fx_in.at[side], device(dx, 0, 0)))
    fy_out[0] = edge_pack(blocks(first), True)
    beside_in = [send(fy_out.at[0], fy_in.at[0], ahead)]
    fy_out[1] = edge_pack(blocks(first), False)
    beside_in.append(send(fy_out.at[1], fy_in.at[1], behind))
    for copy in corner_in + face_in:
        copy.wait_recv()
    assemble(0)
    assemble(X - 1)
    for copy in beside_in:
        copy.wait_recv()
    for x in inner:
        sweep_second(x)
    for copy in first_in:
        copy.wait_recv()
    sweep_second(0)
    sweep_second(X - 1)
    for copy in sent:
        copy.wait_send()


def body(populations, nozzle_mask, wall_type, solid_temp, diffusion, heat_load, coolant_temp):
    sizes = tuple(lax.axis_size(name) for name in ("gx", "gy", "gz"))
    assert sizes[0] > 1 and sizes[1] > 1 and sizes[2] == 2
    _, X, Z, Y = populations.shape
    _, D, W = solid_temp.shape
    assert X >= 2 and W == LANES and Y == sizes[2] * W and Z % ROWS == 0 and D % ROWS == 0
    assert 2 * X * (D // ROWS) <= LANES and len(ACROSS) * X * (Z // ROWS) <= LANES
    rows = -(-len(ACROSS) * X // ROWS) * ROWS
    tall = -(-X // ROWS) * ROWS

    def vmem(*shape):
        return pltpu.VMEM(shape, jnp.float32)

    pair = vmem(2, ROWS, LANES)
    scratch = [
        pltpu.VMEM((X, Y), jnp.int32), pltpu.VMEM((X, Y), jnp.int32), vmem(X, W), vmem(X, W),
        vmem(COUNT, X, Z, Y), vmem(COUNT, X, Z, Y),
        vmem(X, D, W), vmem(X, D, W), vmem(X, D, W),
        vmem(6, X, D, W), vmem(X, D, W), vmem(X, D, W),
        vmem(X, ROWS, Y),
        vmem(2, 2, D, W), pair, pair,
        vmem(tall, W), vmem(tall, W),
        vmem(2, FACE, Z, Y), pair, pair,
        vmem(rows, Y), vmem(rows, Y),
        vmem(2, 2, Z, LANES), vmem(2, ROWS, Y), vmem(2, ROWS, Y),
        vmem(2, tall, LANES), vmem(2, tall, LANES),
        vmem(2, D, W), pair, pair,
        pltpu.SemaphoreType.DMA((X + 6,)),
        pltpu.SemaphoreType.DMA((24,)),
        pltpu.SemaphoreType.DMA((24,)),
    ]
    far = pl.BlockSpec(memory_space=pltpu.HBM)
    local = pl.BlockSpec(memory_space=pltpu.VMEM)
    moved, swept = pl.pallas_call(
        functools.partial(kernel, sizes),
        out_shape=(
            pltpu.VMEM(populations.shape, jnp.float32),
            pltpu.VMEM(solid_temp.shape, jnp.float32),
        ),
        in_specs=[far] * 7,
        out_specs=[local, local],
        scratch_shapes=scratch,
        compiler_params=pltpu.CompilerParams(
            collective_id=0, has_side_effects=True, vmem_limit_bytes=24 * 1024 * 1024
        ),
    )(*(
        pltpu.with_memory_space_constraint(value, pltpu.HBM)
        for value in (populations, solid_temp, diffusion, nozzle_mask, wall_type, heat_load,
                      coolant_temp)
    ))
    return pl.pallas_call(
        deliver,
        out_shape=(
            pltpu.HBM(populations.shape, jnp.float32),
            pltpu.HBM(solid_temp.shape, jnp.float32),
        ),
        in_specs=[pl.BlockSpec(memory_space=pl.ANY)] * 2,
        out_specs=[far, far],
        scratch_shapes=[pltpu.SemaphoreType.DMA((2,))],
        compiler_params=pltpu.CompilerParams(vmem_limit_bytes=1024 * 1024),
    )(*(pltpu.with_memory_space_constraint(value, pltpu.VMEM) for value in (moved, swept)))


def deliver(moved_ref, swept_ref, out_ref, solid_ref, sem):
    copies = [
        pltpu.make_async_copy(moved_ref, out_ref, sem.at[0]),
        pltpu.make_async_copy(swept_ref, solid_ref, sem.at[1]),
    ]
    for copy in copies:
        copy.start()
    for copy in copies:
        copy.wait()


def solution(mesh):
    placed = (
        P(None, "gx", "gz", "gy"),
        P("gx", "gy"),
        P("gx", "gy"),
        P("gx", None, ("gy", "gz")),
        P("gx", None, ("gy", "gz")),
        P("gx", ("gy", "gz")),
        P("gx", ("gy", "gz")),
    )
    return jax.shard_map(
        body,
        mesh=mesh,
        in_specs=placed,
        out_specs=(P(None, "gx", "gz", "gy"), P("gx", None, ("gy", "gz"))),
        check_vma=False,
    )
```

```python
import functools
import jax
import jax.numpy as jnp
import numpy as np
from jax import lax
from jax.experimental import pallas as pl
from jax.experimental.pallas import tpu as pltpu
from jax.sharding import PartitionSpec as P

JET_SPEED = 0.1
H_BASE = 0.5
H_GAIN = 40.0
LANES = 128
ROWS = 8
MESH = pl.DeviceIdType.MESH

VELOCITIES = [
    (0, 0, 0),
    (1, 0, 0), (-1, 0, 0), (0, 1, 0), (0, -1, 0), (0, 0, 1), (0, 0, -1),
    (1, 1, 0), (-1, -1, 0), (1, -1, 0), (-1, 1, 0),
    (1, 0, 1), (-1, 0, -1), (1, 0, -1), (-1, 0, 1),
    (0, 1, 1), (0, -1, -1), (0, 1, -1), (0, -1, 1),
]
COUNT = len(VELOCITIES)
WEIGHTS = [1.0 / 3.0] + [1.0 / 18.0] * 6 + [1.0 / 36.0] * 12
INDEX = {velocity: member for member, velocity in enumerate(VELOCITIES)}
OPPOSITE = [INDEX[(-a, -b, -c)] for a, b, c in VELOCITIES]
ORDER = [i for s in (1, -1, 0) for i in range(COUNT) if VELOCITIES[i][0] == s]
SLOT = {member: place for place, member in enumerate(ORDER)}
FACE = sum(1 for v in VELOCITIES if v[0] == 1)
ACROSS = [(0, 0), (1, 0), (-1, 0), (0, 1), (0, -1)]


def collide(f):
    s = {i: f[i] + f[i + 1] for i in range(1, COUNT, 2)}
    d = {i: f[i] - f[i + 1] for i in range(1, COUNT, 2)}
    jx = (d[1] + d[7]) + (d[9] + d[11]) + d[13]
    jy = (d[3] + d[7]) + (d[15] - d[9]) + d[17]
    jz = (d[5] + d[11]) + (d[15] - d[13]) - d[17]
    sxy, sxz, syz = s[7] + s[9], s[11] + s[13], s[15] + s[17]
    rho = f[0] + (s[1] + s[3] + s[5]) + (sxy + sxz + syz)
    inv = 1.0 / rho
    ux, uy, uz = jx * inv, jy * inv, jz * inv
    px, py, pz = jx * ux, jy * uy, jz * uz
    p = px + py + pz
    base = rho - 1.5 * p
    hxy, hxz, hyz = px + py, px + pz, py + pz
    c4 = 4.0 * f[0] - base
    qxy = c4 + sxy - 2.0 * (s[1] + s[3]) + 0.5 * hxy
    qxz = c4 + sxz - 2.0 * (s[1] + s[5]) + 0.5 * hxz
    qyz = c4 + syz - 2.0 * (s[3] + s[5]) + 0.5 * hyz
    mean = (qxy + qxz + qyz) * (2.0 / 7.0)
    txy, txz, tyz = ((q - mean) * (0.2 / 12.0) for q in (qxy, qxz, qyz))
    post = [None] * COUNT
    post[0] = (1.6 / 3.0) * base - 0.6 * f[0] + 4.0 * (txy + txz + tyz)
    axis_base = (1.6 / 18.0) * base
    for i, pp, tt, j in ((1, px, txy + txz, jx), (3, py, txy + tyz, jy), (5, pz, txz + tyz, jz)):
        even = axis_base + 0.4 * pp - 0.3 * s[i] - 2.0 * tt
        odd = 0.2 * j - 0.1 * d[i]
        post[i], post[i + 1] = even + odd, even - odd
    diag_base = (1.6 / 36.0) * base
    for i, hh, tt, j, k, u in (
        (7, hxy, txy, jx, jy, uy), (11, hxz, txz, jx, jz, uz), (15, hyz, tyz, jy, jz, uz)
    ):
        both = diag_base + 0.2 * hh + tt
        cross = 0.4 * (j * u)
        even = both + cross - 0.3 * s[i]
        odd = 0.1 * (j + k - d[i])
        post[i], post[i + 1] = even + odd, even - odd
        even = both - cross - 0.3 * s[i + 2]
        odd = 0.1 * (j - k - d[i + 2])
        post[i + 2], post[i + 3] = even + odd, even - odd
    return post, p * inv


def lanes_like(shape):
    return lax.broadcasted_iota(jnp.int32, shape, len(shape) - 1)


def rows_like(shape):
    return lax.broadcasted_iota(jnp.int32, shape, len(shape) - 2)


def turned(value, shift, axis):
    shift = shift % value.shape[axis]
    return value if shift == 0 else pltpu.roll(value, shift, axis)


def edge_pack(tiles, last):
    lane = lanes_like((ROWS, LANES))
    packed = jnp.zeros((ROWS, LANES), jnp.float32)
    for k, tile in enumerate(tiles):
        packed = jnp.where(lane == k, turned(tile, k + 1 if last else k, 1), packed)
    return packed


def edge_column(packed, places, last):
    return jnp.concatenate(
        [turned(packed, (LANES - 1 if last else 0) - k, 1) for k in places], axis=0
    )


def kernel(sizes, pops_ref, temp_ref, diff_ref, nozzle_hbm, wall_hbm, load_hbm, cool_hbm,
           out_ref, solid_ref, nozzle_ref, wall_ref, load_ref, cool_ref, pops, post, temp, diff, first, links, base, inverse, heat,
           sx_in, sy_out, sy_in, heat_out, heat_in, px_out, px_in, py_out, py_in, pz_out, pz_in,
           yz_out, yz_in, fx_in, fy_out, fy_in,
           load_sem, send_sem, recv_sem):
    nx, ny, nz = sizes
    gx, gy, gz = (lax.axis_index(name) for name in ("gx", "gy", "gz"))
    X, Z, Y = pops.shape[1:]
    D, W = temp.shape[1:]
    lowest = gz == 0

    def device(dx, dy, other):
        return (lax.rem(gx + dx + nx, nx), lax.rem(gy + dy + ny, ny), 1 - gz if other else gz)

    ahead = (gx, lax.rem(gy + gz, ny), 1 - gz)
    behind = (gx, lax.rem(gy + gz - 1 + ny, ny), 1 - gz)

    near = set()
    for dx, dy, other in (
        [(s, 0, 0) for s in (1, -1)] + [(0, s, 0) for s in (1, -1)] + [(0, 0, 1)]
        + [(0, s, 1) for s in (1, -1)]
    ):
        near.add((dx % nx, dy % ny, other))
    barrier = pltpu.get_barrier_semaphore()
    for dx, dy, other in sorted(near):
        pl.semaphore_signal(
            barrier, inc=1, device_id=device(dx, dy, other), device_id_type=MESH
        )

    loads = [
        pltpu.make_async_copy(temp_ref, temp, load_sem.at[X]),
        pltpu.make_async_copy(diff_ref, diff, load_sem.at[X + 1]),
    ]
    planes = [
        pltpu.make_async_copy(far, near_by, load_sem.at[X + 2 + k])
        for k, (far, near_by) in enumerate((
            (nozzle_hbm, nozzle_ref), (wall_hbm, wall_ref),
            (load_hbm, load_ref), (cool_hbm, cool_ref),
        ))
    ]
    for copy in loads:
        copy.start()
    turn = [X - 1] + list(range(X - 1))
    for x in turn:
        pltpu.make_async_copy(pops_ref.at[:, x], pops.at[:, x], load_sem.at[x]).start()
    for copy in planes:
        copy.start()

    sent = []

    def send(source, target, where):
        place = len(sent)
        copy = pltpu.make_async_remote_copy(
            src_ref=source, dst_ref=target, send_sem=send_sem.at[place],
            recv_sem=recv_sem.at[place], device_id=where, device_id_type=MESH,
        )
        copy.start()
        sent.append(copy)
        return copy

    def blocks(ref):
        return [ref[x, z:z + ROWS, :] for x in range(X) for z in range(0, D, ROWS)]

    pl.semaphore_wait(barrier, len(near))
    sink_in = []
    for side, (edge, dx) in enumerate(((X - 1, 1), (0, -1))):
        sink_in.append(send(temp_ref.at[edge], sx_in.at[side, 0], device(dx, 0, 0)))
        sink_in.append(send(diff_ref.at[edge], sx_in.at[side, 1], device(dx, 0, 0)))

    def collide_plane(step, carry):
        x = lax.rem(step + X - 1, X)
        pltpu.make_async_copy(pops_ref.at[:, x], pops.at[:, x], load_sem.at[x]).wait()
        for z in range(0, Z, ROWS):
            for y in range(0, Y, LANES):
                tile = [pops[i, x, z:z + ROWS, y:y + LANES] for i in range(COUNT)]
                done, square = collide(tile)
                for i in range(COUNT):
                    post[SLOT[i], x, z:z + ROWS, y:y + LANES] = done[i]
                if z == 0:
                    heat[x, :, y:y + LANES] = H_BASE + H_GAIN * square
        return carry

    lax.fori_loop(0, X, collide_plane, 0)
    face_in, edge_in = [], []

    for side, (lane, dy) in enumerate(((Y - LANES, 1), (0, -1))):
        tiles = [
            post[SLOT[INDEX[(a, dy, c)]], x, z:z + ROWS, lane:lane + LANES]
            for a, c in ACROSS for x in range(X) for z in range(0, Z, ROWS)
        ]
        py_out[side] = edge_pack(tiles, dy == 1)
        edge_in.append(send(py_out.at[side], py_in.at[side], device(0, dy, 0)))
    for k, (a, b) in enumerate(ACROSS):
        for x in range(X):
            row = jnp.where(
                lowest,
                post[SLOT[INDEX[(a, b, 1)]], x, Z - 1:Z, :],
                post[SLOT[INDEX[(a, b, -1)]], x, 0:1, :],
            )
            pz_out[k * X + x:k * X + x + 1, :] = row
            if b == 1:
                yz_out[0, x:x + 1, :] = row[:, Y - LANES:]
            if b == -1:
                yz_out[1, x:x + 1, :] = row[:, :LANES]
    edge_in.append(send(pz_out, pz_in, device(0, 0, 1)))
    for side, s in enumerate((1, -1)):
        edge_in.append(send(yz_out.at[side], yz_in.at[side], device(0, s, 1)))

    for x in range(X):
        heat_out[x:x + 1, :] = heat[x, 0:1, W:2 * W]
    heat_copy = send(heat_out, heat_in, device(0, 0, 1))

    for copy in loads:
        copy.wait()
    halved = [0.5 * tile for tile in blocks(diff)]
    sy_out[0] = edge_pack(blocks(temp) + halved, True)
    flank_in = [send(sy_out.at[0], sy_in.at[0], ahead)]
    sy_out[1] = edge_pack(blocks(temp) + halved, False)
    flank_in.append(send(sy_out.at[1], sy_in.at[1], behind))

    lane = lanes_like((D, W))
    depth = rows_like((D, W))
    depth_blocks = D // ROWS
    column = depth_blocks * X

    def beside(value, packs, x, start):
        places = range(start + x * depth_blocks, start + (x + 1) * depth_blocks)
        low = jnp.where(lane == 0, edge_column(packs[0], places, False), turned(value, 1, 1))
        high = jnp.where(
            lane == W - 1, edge_column(packs[1], places, True), turned(value, -1, 1)
        )
        return low, high

    def sweep_first(x):
        own, cond = temp[x], 0.5 * diff[x]
        below = (temp[x - 1], diff[x - 1]) if x > 0 else (sx_in[0, 0], sx_in[0, 1])
        above = (temp[x + 1], diff[x + 1]) if x < X - 1 else (sx_in[1, 0], sx_in[1, 1])
        temps = [below[0], above[0], *beside(own, (sy_in[0], sy_in[1]), x, 0)]
        conds = [0.5 * below[1], 0.5 * above[1], *beside(cond, (sy_in[0], sy_in[1]), x, column)]
        g = [cond + c for c in conds]
        g.append(jnp.where(depth == D - 1, 0.0, cond + turned(cond, -1, 0)))
        g.append(jnp.where(depth == 0, 0.0, cond + turned(cond, 1, 0)))
        temps += [turned(own, -1, 0), turned(own, 1, 0)]
        warm = jnp.where(lowest, heat[x, 0:1, 0:W], heat_in[x:x + 1, :])
        start = own + jnp.where(depth == 0, load_ref[x:x + 1, :], 0.0)
        start = start + jnp.where(depth == D - 1, warm * cool_ref[x:x + 1, :], 0.0)
        denom = 1.0 + jnp.where(depth == D - 1, warm, 0.0)
        numer = start
        for k in range(6):
            numer = numer + g[k] * temps[k]
            denom = denom + g[k]
            links[k, x] = g[k]
        flip = 1.0 / denom
        base[x] = start
        inverse[x] = flip
        first[x] = numer * flip
    wide = lanes_like((Z, Y))
    flat = lanes_like((1, Y))
    level = rows_like((Z, Y))

    def shifted(value, lanes, border, b):
        parts = [border, value[:, LANES:]] if b == 1 else [value[:, :Y - LANES], border]
        edge = jnp.concatenate(parts, axis=1)
        spot = 0 if b == 1 else Y - 1
        return jnp.where(lanes == spot, edge, turned(value, b, 1))

    tall = Z // ROWS

    floor = level == jnp.where(lowest, 0, -1)
    roof = level == jnp.where(lowest, -1, Z - 1)

    def move(i, source):
        a, b, c = VELOCITIES[i]
        value = post[SLOT[i], source]
        if b != 0:
            flank = 0 if b == 1 else 1
            begin = (ACROSS.index((a, c)) * X + source) * tall
            border = edge_column(py_in[flank], range(begin, begin + tall), b == -1)
            value = shifted(value, wide, border, b)
        if c != 0:
            at = ACROSS.index((a, b)) * X + source
            row = pz_in[at:at + 1, :]
            if b != 0:
                row = shifted(row, flat, turned(yz_in[flank], b, 1)[source:source + 1, :], b)
            value = jnp.where(level == (0 if c == 1 else Z - 1), row, turned(value, c, 0))
        return value

    def assemble(x, members):
        nozzle = nozzle_ref[x:x + 1, :] == 1
        outlet = wall_ref[x:x + 1, :] == 1
        for i in members:
            a, b, c = VELOCITIES[i]
            if 0 <= x - a < X:
                value = move(i, x - a)
            else:
                side = 0 if a == 1 else 1
                value = px_in[side, SLOT[i] - side * FACE]
            back = SLOT[OPPOSITE[i]]
            if c == 1:
                value = jnp.where(floor, post[back, x, 0:1, :], value)
            if c == -1:
                closed = post[back, x, Z - 1:Z, :]
                jet = closed + 6.0 * WEIGHTS[i] * JET_SPEED
                plate = jnp.where(
                    nozzle, jet, jnp.where(outlet, post[SLOT[i], x, Z - 1:Z, :], closed)
                )
                value = jnp.where(roof, plate, value)
            out_ref[i, x] = value

    def sweep_second(x):
        own = first[x]
        below = first[x - 1] if x > 0 else fx_in[0]
        above = first[x + 1] if x < X - 1 else fx_in[1]
        sides = beside(own, (fy_in[0], fy_in[1]), x, 0)
        temps = [below, above, *sides, turned(own, -1, 0), turned(own, 1, 0)]
        numer = base[x]
        for k in range(6):
            numer = numer + links[k, x] * temps[k]
        solid_ref[x] = numer * inverse[x]

    inner = range(1, X - 1)
    own = {x: [i for i in range(COUNT) if 0 <= x - VELOCITIES[i][0] < X] for x in range(X)}
    for copy in edge_in:
        copy.wait_recv()
    for side, (edge, dx) in enumerate(((X - 1, 1), (0, -1))):
        for k in range(FACE):
            px_out[side, k] = move(ORDER[side * FACE + k], edge)
        face_in.append(send(px_out.at[side], px_in.at[side], device(dx, 0, 0)))
    for copy in planes:
        copy.wait()
    for copy in flank_in + [heat_copy]:
        copy.wait_recv()
    for x in inner:
        sweep_first(x)
    for copy in sink_in:
        copy.wait_recv()
    first_in = []
    for side, (edge, dx) in enumerate(((X - 1, 1), (0, -1))):
        sweep_first(edge)
        first_in.append(send(first.at[edge], fx_in.at[side], device(dx, 0, 0)))
    fy_out[0] = edge_pack(blocks(first), True)
    beside_in = [send(fy_out.at[0], fy_in.at[0], ahead)]
    fy_out[1] = edge_pack(blocks(first), False)
    beside_in.append(send(fy_out.at[1], fy_in.at[1], behind))
    for x in range(X):
        assemble(x, own[x])
    for copy in beside_in:
        copy.wait_recv()
    for x in inner:
        sweep_second(x)
    for copy in first_in:
        copy.wait_recv()
    sweep_second(0)
    sweep_second(X - 1)
    for copy in face_in:
        copy.wait_recv()
    for x in (0, X - 1):
        assemble(x, [i for i in range(COUNT) if i not in own[x]])
    for copy in sent:
        copy.wait_send()


def body(populations, nozzle_mask, wall_type, solid_temp, diffusion, heat_load, coolant_temp):
    sizes = tuple(lax.axis_size(name) for name in ("gx", "gy", "gz"))
    assert sizes[0] > 1 and sizes[1] > 1 and sizes[2] == 2
    _, X, Z, Y = populations.shape
    _, D, W = solid_temp.shape
    assert X >= 2 and W == LANES and Y == sizes[2] * W and Z % ROWS == 0 and D % ROWS == 0
    assert 2 * X * (D // ROWS) <= LANES and len(ACROSS) * X * (Z // ROWS) <= LANES
    rows = -(-len(ACROSS) * X // ROWS) * ROWS
    tall = -(-X // ROWS) * ROWS

    def vmem(*shape):
        return pltpu.VMEM(shape, jnp.float32)

    pair = vmem(2, ROWS, LANES)
    scratch = [
        pltpu.VMEM((X, Y), jnp.int32), pltpu.VMEM((X, Y), jnp.int32), vmem(X, W), vmem(X, W),
        vmem(COUNT, X, Z, Y), vmem(COUNT, X, Z, Y),
        vmem(X, D, W), vmem(X, D, W), vmem(X, D, W),
        vmem(6, X, D, W), vmem(X, D, W), vmem(X, D, W),
        vmem(X, ROWS, Y),
        vmem(2, 2, D, W), pair, pair,
        vmem(tall, W), vmem(tall, W),
        vmem(2, FACE, Z, Y), vmem(2, FACE, Z, Y), pair, pair,
        vmem(rows, Y), vmem(rows, Y),
        vmem(2, tall, LANES), vmem(2, tall, LANES),
        vmem(2, D, W), pair, pair,
        pltpu.SemaphoreType.DMA((X + 6,)),
        pltpu.SemaphoreType.DMA((18,)),
        pltpu.SemaphoreType.DMA((18,)),
    ]
    far = pl.BlockSpec(memory_space=pltpu.HBM)
    local = pl.BlockSpec(memory_space=pltpu.VMEM)
    moved, swept = pl.pallas_call(
        functools.partial(kernel, sizes),
        out_shape=(
            pltpu.VMEM(populations.shape, jnp.float32),
            pltpu.VMEM(solid_temp.shape, jnp.float32),
        ),
        in_specs=[far] * 7,
        out_specs=[local, local],
        scratch_shapes=scratch,
        compiler_params=pltpu.CompilerParams(
            collective_id=0, has_side_effects=True, vmem_limit_bytes=24 * 1024 * 1024
        ),
    )(*(
        pltpu.with_memory_space_constraint(value, pltpu.HBM)
        for value in (populations, solid_temp, diffusion, nozzle_mask, wall_type, heat_load,
                      coolant_temp)
    ))
    return pl.pallas_call(
        deliver,
        out_shape=(
            pltpu.HBM(populations.shape, jnp.float32),
            pltpu.HBM(solid_temp.shape, jnp.float32),
        ),
        in_specs=[pl.BlockSpec(memory_space=pl.ANY)] * 2,
        out_specs=[far, far],
        scratch_shapes=[pltpu.SemaphoreType.DMA((2,))],
        compiler_params=pltpu.CompilerParams(vmem_limit_bytes=1024 * 1024),
    )(*(pltpu.with_memory_space_constraint(value, pltpu.VMEM) for value in (moved, swept)))


def deliver(moved_ref, swept_ref, out_ref, solid_ref, sem):
    copies = [
        pltpu.make_async_copy(moved_ref, out_ref, sem.at[0]),
        pltpu.make_async_copy(swept_ref, solid_ref, sem.at[1]),
    ]
    for copy in copies:
        copy.start()
    for copy in copies:
        copy.wait()


def solution(mesh):
    placed = (
        P(None, "gx", "gz", "gy"),
        P("gx", "gy"),
        P("gx", "gy"),
        P("gx", None, ("gy", "gz")),
        P("gx", None, ("gy", "gz")),
        P("gx", ("gy", "gz")),
        P("gx", ("gy", "gz")),
    )
    return jax.shard_map(
        body,
        mesh=mesh,
        in_specs=placed,
        out_specs=(P(None, "gx", "gz", "gy"), P("gx", None, ("gy", "gz"))),
        check_vma=False,
    )
```

```python
import functools
import jax
import jax.numpy as jnp
import numpy as np
from jax import lax
from jax.experimental import pallas as pl
from jax.experimental.pallas import tpu as pltpu
from jax.sharding import PartitionSpec as P

JET_SPEED = 0.1
H_BASE = 0.5
H_GAIN = 40.0
LANES = 128
ROWS = 8
MESH = pl.DeviceIdType.MESH

VELOCITIES = [
    (0, 0, 0),
    (1, 0, 0), (-1, 0, 0), (0, 1, 0), (0, -1, 0), (0, 0, 1), (0, 0, -1),
    (1, 1, 0), (-1, -1, 0), (1, -1, 0), (-1, 1, 0),
    (1, 0, 1), (-1, 0, -1), (1, 0, -1), (-1, 0, 1),
    (0, 1, 1), (0, -1, -1), (0, 1, -1), (0, -1, 1),
]
COUNT = len(VELOCITIES)
WEIGHTS = [1.0 / 3.0] + [1.0 / 18.0] * 6 + [1.0 / 36.0] * 12
INDEX = {velocity: member for member, velocity in enumerate(VELOCITIES)}
OPPOSITE = [INDEX[(-a, -b, -c)] for a, b, c in VELOCITIES]
ORDER = [i for s in (1, -1, 0) for i in range(COUNT) if VELOCITIES[i][0] == s]
SLOT = {member: place for place, member in enumerate(ORDER)}
FACE = sum(1 for v in VELOCITIES if v[0] == 1)
ACROSS = [(0, 0), (1, 0), (-1, 0), (0, 1), (0, -1)]


def collide(f):
    s = {i: f[i] + f[i + 1] for i in range(1, COUNT, 2)}
    d = {i: f[i] - f[i + 1] for i in range(1, COUNT, 2)}
    jx = (d[1] + d[7]) + (d[9] + d[11]) + d[13]
    jy = (d[3] + d[7]) + (d[15] - d[9]) + d[17]
    jz = (d[5] + d[11]) + (d[15] - d[13]) - d[17]
    sxy, sxz, syz = s[7] + s[9], s[11] + s[13], s[15] + s[17]
    rho = f[0] + (s[1] + s[3] + s[5]) + (sxy + sxz + syz)
    inv = 1.0 / rho
    ux, uy, uz = jx * inv, jy * inv, jz * inv
    px, py, pz = jx * ux, jy * uy, jz * uz
    p = px + py + pz
    base = rho - 1.5 * p
    hxy, hxz, hyz = px + py, px + pz, py + pz
    c4 = 4.0 * f[0] - base
    qxy = c4 + sxy - 2.0 * (s[1] + s[3]) + 0.5 * hxy
    qxz = c4 + sxz - 2.0 * (s[1] + s[5]) + 0.5 * hxz
    qyz = c4 + syz - 2.0 * (s[3] + s[5]) + 0.5 * hyz
    mean = (qxy + qxz + qyz) * (2.0 / 7.0)
    txy, txz, tyz = ((q - mean) * (0.2 / 12.0) for q in (qxy, qxz, qyz))
    post = [None] * COUNT
    post[0] = (1.6 / 3.0) * base - 0.6 * f[0] + 4.0 * (txy + txz + tyz)
    axis_base = (1.6 / 18.0) * base
    for i, pp, tt, j in ((1, px, txy + txz, jx), (3, py, txy + tyz, jy), (5, pz, txz + tyz, jz)):
        even = axis_base + 0.4 * pp - 0.3 * s[i] - 2.0 * tt
        odd = 0.2 * j - 0.1 * d[i]
        post[i], post[i + 1] = even + odd, even - odd
    diag_base = (1.6 / 36.0) * base
    for i, hh, tt, j, k, u in (
        (7, hxy, txy, jx, jy, uy), (11, hxz, txz, jx, jz, uz), (15, hyz, tyz, jy, jz, uz)
    ):
        both = diag_base + 0.2 * hh + tt
        cross = 0.4 * (j * u)
        even = both + cross - 0.3 * s[i]
        odd = 0.1 * (j + k - d[i])
        post[i], post[i + 1] = even + odd, even - odd
        even = both - cross - 0.3 * s[i + 2]
        odd = 0.1 * (j - k - d[i + 2])
        post[i + 2], post[i + 3] = even + odd, even - odd
    return post, p * inv


def lanes_like(shape):
    return lax.broadcasted_iota(jnp.int32, shape, len(shape) - 1)


def rows_like(shape):
    return lax.broadcasted_iota(jnp.int32, shape, len(shape) - 2)


def turned(value, shift, axis):
    size = value.shape[axis]
    if isinstance(shift, int):
        shift = shift % size
        return value if shift == 0 else pltpu.roll(value, shift, axis)
    return pltpu.roll(value, lax.rem(shift + size, size), axis)


def edge_pack(tiles, last):
    lane = lanes_like((ROWS, LANES))
    packed = jnp.zeros((ROWS, LANES), jnp.float32)
    for k, tile in enumerate(tiles):
        packed = jnp.where(lane == k, turned(tile, k + 1 if last else k, 1), packed)
    return packed


def edge_column(packed, places, last):
    return jnp.concatenate(
        [turned(packed, (LANES - 1 if last else 0) - k, 1) for k in places], axis=0
    )


def kernel(sizes, pops_ref, temp_ref, diff_ref, nozzle_hbm, wall_hbm, load_hbm, cool_hbm,
           out_ref, solid_ref, nozzle_ref, wall_ref, load_ref, cool_ref, pops, post, temp, diff, first, links, base, inverse, heat,
           sy_out, sy_in, heat_out, heat_in, px_out, px_in, py_out, py_in, pz_out, pz_in,
           yz_out, yz_in, fy_out, fy_in,
           load_sem, send_sem, recv_sem):
    nx, ny, nz = sizes
    gx, gy, gz = (lax.axis_index(name) for name in ("gx", "gy", "gz"))
    X, Z, Y = pops.shape[1:]
    D, W = temp.shape[1:]
    lowest = gz == 0

    def device(dx, dy, other):
        return (lax.rem(gx + dx + nx, nx), lax.rem(gy + dy + ny, ny), 1 - gz if other else gz)

    ahead = (gx, lax.rem(gy + gz, ny), 1 - gz)
    behind = (gx, lax.rem(gy + gz - 1 + ny, ny), 1 - gz)

    near = set()
    for dx, dy, other in (
        [(s, 0, 0) for s in (1, -1)] + [(0, s, 0) for s in (1, -1)] + [(0, 0, 1)]
        + [(0, s, 1) for s in (1, -1)]
    ):
        near.add((dx % nx, dy % ny, other))
    barrier = pltpu.get_barrier_semaphore()
    for dx, dy, other in sorted(near):
        pl.semaphore_signal(
            barrier, inc=1, device_id=device(dx, dy, other), device_id_type=MESH
        )

    loads = [
        pltpu.make_async_copy(temp_ref, temp.at[pl.ds(1, X)], load_sem.at[X]),
        pltpu.make_async_copy(diff_ref, diff.at[pl.ds(1, X)], load_sem.at[X + 1]),
    ]
    planes = [
        pltpu.make_async_copy(far, near_by, load_sem.at[X + 2 + k])
        for k, (far, near_by) in enumerate((
            (nozzle_hbm, nozzle_ref), (wall_hbm, wall_ref),
            (load_hbm, load_ref), (cool_hbm, cool_ref),
        ))
    ]
    for copy in loads:
        copy.start()
    turn = [X - 1] + list(range(X - 1))
    for x in turn:
        pltpu.make_async_copy(pops_ref.at[:, x], pops.at[:, x], load_sem.at[x]).start()
    for copy in planes:
        copy.start()

    sent = []

    def send(source, target, where):
        place = len(sent)
        copy = pltpu.make_async_remote_copy(
            src_ref=source, dst_ref=target, send_sem=send_sem.at[place],
            recv_sem=recv_sem.at[place], device_id=where, device_id_type=MESH,
        )
        copy.start()
        sent.append(copy)
        return copy

    def blocks(ref):
        return [ref[1 + x, z:z + ROWS, :] for x in range(X) for z in range(0, D, ROWS)]

    pl.semaphore_wait(barrier, len(near))
    sink_in = []
    for edge, slot, dx in ((X - 1, 0, 1), (0, X + 1, -1)):
        sink_in.append(send(temp_ref.at[edge], temp.at[slot], device(dx, 0, 0)))
        sink_in.append(send(diff_ref.at[edge], diff.at[slot], device(dx, 0, 0)))

    def collide_plane(step, carry):
        x = lax.rem(step + X - 1, X)
        pltpu.make_async_copy(pops_ref.at[:, x], pops.at[:, x], load_sem.at[x]).wait()
        for z in range(0, Z, ROWS):
            for y in range(0, Y, LANES):
                tile = [pops[i, x, z:z + ROWS, y:y + LANES] for i in range(COUNT)]
                done, square = collide(tile)
                for i in range(COUNT):
                    post[SLOT[i], x, z:z + ROWS, y:y + LANES] = done[i]
                if z == 0:
                    heat[x, :, y:y + LANES] = H_BASE + H_GAIN * square
        return carry

    lax.fori_loop(0, X, collide_plane, 0)
    face_in, edge_in = [], []

    for side, (lane, dy) in enumerate(((Y - LANES, 1), (0, -1))):
        tiles = [
            post[SLOT[INDEX[(a, dy, c)]], x, z:z + ROWS, lane:lane + LANES]
            for a, c in ACROSS for x in range(X) for z in range(0, Z, ROWS)
        ]
        py_out[side] = edge_pack(tiles, dy == 1)
        edge_in.append(send(py_out.at[side], py_in.at[side], device(0, dy, 0)))
    for k, (a, b) in enumerate(ACROSS):
        for x in range(X):
            row = jnp.where(
                lowest,
                post[SLOT[INDEX[(a, b, 1)]], x, Z - 1:Z, :],
                post[SLOT[INDEX[(a, b, -1)]], x, 0:1, :],
            )
            pz_out[k * X + x:k * X + x + 1, :] = row
            if b == 1:
                yz_out[0, x:x + 1, :] = row[:, Y - LANES:]
            if b == -1:
                yz_out[1, x:x + 1, :] = row[:, :LANES]
    edge_in.append(send(pz_out, pz_in, device(0, 0, 1)))
    for side, s in enumerate((1, -1)):
        edge_in.append(send(yz_out.at[side], yz_in.at[side], device(0, s, 1)))

    for x in range(X):
        heat_out[x:x + 1, :] = heat[x, 0:1, W:2 * W]
    heat_copy = send(heat_out, heat_in, device(0, 0, 1))

    for copy in loads:
        copy.wait()
    halved = [0.5 * tile for tile in blocks(diff)]
    sy_out[0] = edge_pack(blocks(temp) + halved, True)
    flank_in = [send(sy_out.at[0], sy_in.at[0], ahead)]
    sy_out[1] = edge_pack(blocks(temp) + halved, False)
    flank_in.append(send(sy_out.at[1], sy_in.at[1], behind))

    lane = lanes_like((D, W))
    depth = rows_like((D, W))
    depth_blocks = D // ROWS
    column = depth_blocks * X

    def beside(value, packs, x, start):
        places = [start + x * depth_blocks + k for k in range(depth_blocks)]
        low = jnp.where(lane == 0, edge_column(packs[0], places, False), turned(value, 1, 1))
        high = jnp.where(
            lane == W - 1, edge_column(packs[1], places, True), turned(value, -1, 1)
        )
        return low, high

    def sweep_first(x, carry):
        own, cond = temp[x + 1], 0.5 * diff[x + 1]
        below, above = (temp[x], diff[x]), (temp[x + 2], diff[x + 2])
        temps = [below[0], above[0], *beside(own, (sy_in[0], sy_in[1]), x, 0)]
        conds = [0.5 * below[1], 0.5 * above[1], *beside(cond, (sy_in[0], sy_in[1]), x, column)]
        g = [cond + c for c in conds]
        g.append(jnp.where(depth == D - 1, 0.0, cond + turned(cond, -1, 0)))
        g.append(jnp.where(depth == 0, 0.0, cond + turned(cond, 1, 0)))
        temps += [turned(own, -1, 0), turned(own, 1, 0)]
        warm = jnp.where(lowest, heat[x, 0:1, 0:W], heat_in[pl.ds(x, 1), :])
        start = own + jnp.where(depth == 0, load_ref[pl.ds(x, 1), :], 0.0)
        start = start + jnp.where(depth == D - 1, warm * cool_ref[pl.ds(x, 1), :], 0.0)
        denom = 1.0 + jnp.where(depth == D - 1, warm, 0.0)
        numer = start
        for k in range(6):
            numer = numer + g[k] * temps[k]
            denom = denom + g[k]
            links[k, x] = g[k]
        flip = 1.0 / denom
        base[x] = start
        inverse[x] = flip
        first[x + 1] = numer * flip
        return carry

    wide = lanes_like((Z, Y))
    flat = lanes_like((1, Y))
    level = rows_like((Z, Y))

    def shifted(value, lanes, border, b):
        parts = [border, value[:, LANES:]] if b == 1 else [value[:, :Y - LANES], border]
        edge = jnp.concatenate(parts, axis=1)
        spot = 0 if b == 1 else Y - 1
        return jnp.where(lanes == spot, edge, turned(value, b, 1))

    tall = Z // ROWS

    floor = level == jnp.where(lowest, 0, -1)
    roof = level == jnp.where(lowest, -1, Z - 1)

    def move(i, source):
        a, b, c = VELOCITIES[i]
        value = post[SLOT[i], source]
        if b != 0:
            flank = 0 if b == 1 else 1
            begin = (ACROSS.index((a, c)) * X + source) * tall
            places = [begin + k for k in range(tall)]
            border = edge_column(py_in[flank], places, b == -1)
            value = shifted(value, wide, border, b)
        if c != 0:
            row = pz_in[pl.ds(ACROSS.index((a, b)) * X + source, 1), :]
            if b != 0:
                row = shifted(row, flat, turned(yz_in[flank, pl.ds(source, 1), :], b, 1), b)
            value = jnp.where(level == (0 if c == 1 else Z - 1), row, turned(value, c, 0))
        return value

    def assemble(x, carry):
        for i, (a, _, _) in enumerate(VELOCITIES):
            source = x if a == 0 else jnp.clip(x - a, 0, X - 1)
            settle(i, x, move(i, source))
        return carry

    def settle(i, x, value):
        c = VELOCITIES[i][2]
        back = SLOT[OPPOSITE[i]]
        if c == 1:
            value = jnp.where(floor, post[back, x, 0:1, :], value)
        if c == -1:
            closed = post[back, x, Z - 1:Z, :]
            jet = closed + 6.0 * WEIGHTS[i] * JET_SPEED
            open_value = post[SLOT[i], x, Z - 1:Z, :]
            nozzle = nozzle_ref[pl.ds(x, 1), :] == 1
            outlet = wall_ref[pl.ds(x, 1), :] == 1
            plate = jnp.where(nozzle, jet, jnp.where(outlet, open_value, closed))
            value = jnp.where(roof, plate, value)
        out_ref[i, x] = value

    def sweep_second(x, carry):
        own, below, above = first[x + 1], first[x], first[x + 2]
        sides = beside(own, (fy_in[0], fy_in[1]), x, 0)
        temps = [below, above, *sides, turned(own, -1, 0), turned(own, 1, 0)]
        numer = base[x]
        for k in range(6):
            numer = numer + links[k, x] * temps[k]
        solid_ref[x] = numer * inverse[x]
        return carry

    for copy in edge_in:
        copy.wait_recv()
    for side, (edge, dx) in enumerate(((X - 1, 1), (0, -1))):
        for k in range(FACE):
            px_out[side, k] = move(ORDER[side * FACE + k], edge)
        face_in.append(send(px_out.at[side], px_in.at[side], device(dx, 0, 0)))
    for copy in planes:
        copy.wait()
    for copy in flank_in + [heat_copy]:
        copy.wait_recv()
    lax.fori_loop(1, X - 1, sweep_first, 0)
    for copy in sink_in:
        copy.wait_recv()
    first_in = []
    lax.fori_loop(0, 2, lambda k, carry: sweep_first(k * (X - 1), carry), 0)
    for edge, slot, dx in ((X, 0, 1), (1, X + 1, -1)):
        first_in.append(send(first.at[edge], first.at[slot], device(dx, 0, 0)))
    fy_out[0] = edge_pack(blocks(first), True)
    beside_in = [send(fy_out.at[0], fy_in.at[0], ahead)]
    fy_out[1] = edge_pack(blocks(first), False)
    beside_in.append(send(fy_out.at[1], fy_in.at[1], behind))
    lax.fori_loop(0, X, assemble, 0)
    for copy in beside_in:
        copy.wait_recv()
    for copy in first_in:
        copy.wait_recv()
    lax.fori_loop(0, X, sweep_second, 0)
    for copy in face_in:
        copy.wait_recv()
    for side, x in enumerate((0, X - 1)):
        for k in range(FACE):
            settle(ORDER[side * FACE + k], x, px_in[side, k])
    for copy in sent:
        copy.wait_send()


def body(populations, nozzle_mask, wall_type, solid_temp, diffusion, heat_load, coolant_temp):
    sizes = tuple(lax.axis_size(name) for name in ("gx", "gy", "gz"))
    assert sizes[0] > 1 and sizes[1] > 1 and sizes[2] == 2
    _, X, Z, Y = populations.shape
    _, D, W = solid_temp.shape
    assert X >= 2 and W == LANES and Y == sizes[2] * W and Z % ROWS == 0 and D % ROWS == 0
    assert 2 * X * (D // ROWS) <= LANES and len(ACROSS) * X * (Z // ROWS) <= LANES
    rows = -(-len(ACROSS) * X // ROWS) * ROWS
    tall = -(-X // ROWS) * ROWS

    def vmem(*shape):
        return pltpu.VMEM(shape, jnp.float32)

    pair = vmem(2, ROWS, LANES)
    scratch = [
        pltpu.VMEM((X, Y), jnp.int32), pltpu.VMEM((X, Y), jnp.int32), vmem(X, W), vmem(X, W),
        vmem(COUNT, X, Z, Y), vmem(COUNT, X, Z, Y),
        vmem(X + 2, D, W), vmem(X + 2, D, W), vmem(X + 2, D, W),
        vmem(6, X, D, W), vmem(X, D, W), vmem(X, D, W),
        vmem(X, ROWS, Y),
        pair, pair,
        vmem(tall, W), vmem(tall, W),
        vmem(2, FACE, Z, Y), vmem(2, FACE, Z, Y), pair, pair,
        vmem(rows, Y), vmem(rows, Y),
        vmem(2, tall, LANES), vmem(2, tall, LANES),
        pair, pair,
        pltpu.SemaphoreType.DMA((X + 6,)),
        pltpu.SemaphoreType.DMA((18,)),
        pltpu.SemaphoreType.DMA((18,)),
    ]
    far = pl.BlockSpec(memory_space=pltpu.HBM)
    local = pl.BlockSpec(memory_space=pltpu.VMEM)
    moved, swept = pl.pallas_call(
        functools.partial(kernel, sizes),
        out_shape=(
            pltpu.VMEM(populations.shape, jnp.float32),
            pltpu.VMEM(solid_temp.shape, jnp.float32),
        ),
        in_specs=[far] * 7,
        out_specs=[local, local],
        scratch_shapes=scratch,
        compiler_params=pltpu.CompilerParams(
            collective_id=0, has_side_effects=True, vmem_limit_bytes=24 * 1024 * 1024
        ),
    )(*(
        pltpu.with_memory_space_constraint(value, pltpu.HBM)
        for value in (populations, solid_temp, diffusion, nozzle_mask, wall_type, heat_load,
                      coolant_temp)
    ))
    return pl.pallas_call(
        deliver,
        out_shape=(
            pltpu.HBM(populations.shape, jnp.float32),
            pltpu.HBM(solid_temp.shape, jnp.float32),
        ),
        in_specs=[pl.BlockSpec(memory_space=pl.ANY)] * 2,
        out_specs=[far, far],
        scratch_shapes=[pltpu.SemaphoreType.DMA((populations.shape[1] + 1,))],
        compiler_params=pltpu.CompilerParams(vmem_limit_bytes=1024 * 1024),
    )(*(pltpu.with_memory_space_constraint(value, pltpu.VMEM) for value in (moved, swept)))


def deliver(moved_ref, swept_ref, out_ref, solid_ref, sem):
    planes = moved_ref.shape[1]
    copies = [pltpu.make_async_copy(swept_ref, solid_ref, sem.at[planes])]
    for x in range(planes):
        copies.append(pltpu.make_async_copy(moved_ref.at[:, x], out_ref.at[:, x], sem.at[x]))
    for copy in copies:
        copy.start()
    for copy in copies:
        copy.wait()


def solution(mesh):
    placed = (
        P(None, "gx", "gz", "gy"),
        P("gx", "gy"),
        P("gx", "gy"),
        P("gx", None, ("gy", "gz")),
        P("gx", None, ("gy", "gz")),
        P("gx", ("gy", "gz")),
        P("gx", ("gy", "gz")),
    )
    return jax.shard_map(
        body,
        mesh=mesh,
        in_specs=placed,
        out_specs=(P(None, "gx", "gz", "gy"), P("gx", None, ("gy", "gz"))),
        check_vma=False,
    )
```

```python
import functools
import jax
import jax.numpy as jnp
import numpy as np
from jax import lax
from jax.experimental import pallas as pl
from jax.experimental.pallas import tpu as pltpu
from jax.sharding import PartitionSpec as P

JET_SPEED = 0.1
H_BASE = 0.5
H_GAIN = 40.0
LANES = 128
ROWS = 8
MESH = pl.DeviceIdType.MESH

VELOCITIES = [
    (0, 0, 0),
    (1, 0, 0), (-1, 0, 0), (0, 1, 0), (0, -1, 0), (0, 0, 1), (0, 0, -1),
    (1, 1, 0), (-1, -1, 0), (1, -1, 0), (-1, 1, 0),
    (1, 0, 1), (-1, 0, -1), (1, 0, -1), (-1, 0, 1),
    (0, 1, 1), (0, -1, -1), (0, 1, -1), (0, -1, 1),
]
COUNT = len(VELOCITIES)
WEIGHTS = [1.0 / 3.0] + [1.0 / 18.0] * 6 + [1.0 / 36.0] * 12
INDEX = {velocity: member for member, velocity in enumerate(VELOCITIES)}
OPPOSITE = [INDEX[(-a, -b, -c)] for a, b, c in VELOCITIES]
ORDER = [i for s in (1, -1, 0) for i in range(COUNT) if VELOCITIES[i][0] == s]
SLOT = {member: place for place, member in enumerate(ORDER)}
FACE = sum(1 for v in VELOCITIES if v[0] == 1)
ACROSS = [(0, 0), (1, 0), (-1, 0), (0, 1), (0, -1)]


def collide(f):
    s = {i: f[i] + f[i + 1] for i in range(1, COUNT, 2)}
    d = {i: f[i] - f[i + 1] for i in range(1, COUNT, 2)}
    jx = (d[1] + d[7]) + (d[9] + d[11]) + d[13]
    jy = (d[3] + d[7]) + (d[15] - d[9]) + d[17]
    jz = (d[5] + d[11]) + (d[15] - d[13]) - d[17]
    sxy, sxz, syz = s[7] + s[9], s[11] + s[13], s[15] + s[17]
    rho = f[0] + (s[1] + s[3] + s[5]) + (sxy + sxz + syz)
    inv = 1.0 / rho
    ux, uy, uz = jx * inv, jy * inv, jz * inv
    px, py, pz = jx * ux, jy * uy, jz * uz
    p = px + py + pz
    base = rho - 1.5 * p
    hxy, hxz, hyz = px + py, px + pz, py + pz
    c4 = 4.0 * f[0] - base
    qxy = c4 + sxy - 2.0 * (s[1] + s[3]) + 0.5 * hxy
    qxz = c4 + sxz - 2.0 * (s[1] + s[5]) + 0.5 * hxz
    qyz = c4 + syz - 2.0 * (s[3] + s[5]) + 0.5 * hyz
    mean = (qxy + qxz + qyz) * (2.0 / 7.0)
    txy, txz, tyz = ((q - mean) * (0.2 / 12.0) for q in (qxy, qxz, qyz))
    post = [None] * COUNT
    post[0] = (1.6 / 3.0) * base - 0.6 * f[0] + 4.0 * (txy + txz + tyz)
    axis_base = (1.6 / 18.0) * base
    for i, pp, tt, j in ((1, px, txy + txz, jx), (3, py, txy + tyz, jy), (5, pz, txz + tyz, jz)):
        even = axis_base + 0.4 * pp - 0.3 * s[i] - 2.0 * tt
        odd = 0.2 * j - 0.1 * d[i]
        post[i], post[i + 1] = even + odd, even - odd
    diag_base = (1.6 / 36.0) * base
    for i, hh, tt, j, k, u in (
        (7, hxy, txy, jx, jy, uy), (11, hxz, txz, jx, jz, uz), (15, hyz, tyz, jy, jz, uz)
    ):
        both = diag_base + 0.2 * hh + tt
        cross = 0.4 * (j * u)
        even = both + cross - 0.3 * s[i]
        odd = 0.1 * (j + k - d[i])
        post[i], post[i + 1] = even + odd, even - odd
        even = both - cross - 0.3 * s[i + 2]
        odd = 0.1 * (j - k - d[i + 2])
        post[i + 2], post[i + 3] = even + odd, even - odd
    return post, p * inv


def lanes_like(shape):
    return lax.broadcasted_iota(jnp.int32, shape, len(shape) - 1)


def rows_like(shape):
    return lax.broadcasted_iota(jnp.int32, shape, len(shape) - 2)


def turned(value, shift, axis):
    shift = shift % value.shape[axis]
    return value if shift == 0 else pltpu.roll(value, shift, axis)


def edge_pack(tiles, last):
    lane = lanes_like((ROWS, LANES))
    packed = jnp.zeros((ROWS, LANES), jnp.float32)
    for k, tile in enumerate(tiles):
        packed = jnp.where(lane == k, turned(tile, k + 1 if last else k, 1), packed)
    return packed


def edge_column(packed, places, last):
    return jnp.concatenate(
        [turned(packed, (LANES - 1 if last else 0) - k, 1) for k in places], axis=0
    )


def kernel(sizes, pops_ref, temp_ref, diff_ref, nozzle_hbm, wall_hbm, load_hbm, cool_hbm,
           out_ref, solid_ref, nozzle_ref, wall_ref, load_ref, cool_ref, pops, post, temp, diff, first, links, base, inverse, heat,
           sx_in, sy_out, sy_in, heat_out, heat_in, px_out, px_in, py_out, py_in, pz_out, pz_in,
           yz_out, yz_in, fx_in, fy_out, fy_in,
           load_sem, send_sem, recv_sem):
    nx, ny, nz = sizes
    gx, gy, gz = (lax.axis_index(name) for name in ("gx", "gy", "gz"))
    X, Z, Y = pops.shape[1:]
    D, W = temp.shape[1:]
    lowest = gz == 0

    def device(dx, dy, other):
        return (lax.rem(gx + dx + nx, nx), lax.rem(gy + dy + ny, ny), 1 - gz if other else gz)

    ahead = (gx, lax.rem(gy + gz, ny), 1 - gz)
    behind = (gx, lax.rem(gy + gz - 1 + ny, ny), 1 - gz)

    near = set()
    for dx, dy, other in (
        [(s, 0, 0) for s in (1, -1)] + [(0, s, 0) for s in (1, -1)] + [(0, 0, 1)]
        + [(0, s, 1) for s in (1, -1)]
    ):
        near.add((dx % nx, dy % ny, other))
    barrier = pltpu.get_barrier_semaphore()
    for dx, dy, other in sorted(near):
        pl.semaphore_signal(
            barrier, inc=1, device_id=device(dx, dy, other), device_id_type=MESH
        )

    loads = [
        pltpu.make_async_copy(temp_ref, temp, load_sem.at[X]),
        pltpu.make_async_copy(diff_ref, diff, load_sem.at[X + 1]),
    ]
    planes = [
        pltpu.make_async_copy(far, near_by, load_sem.at[X + 2 + k])
        for k, (far, near_by) in enumerate((
            (nozzle_hbm, nozzle_ref), (wall_hbm, wall_ref),
            (load_hbm, load_ref), (cool_hbm, cool_ref),
        ))
    ]
    for copy in loads:
        copy.start()
    turn = [X - 1] + list(range(X - 1))
    for x in turn:
        pltpu.make_async_copy(pops_ref.at[:, x], pops.at[:, x], load_sem.at[x]).start()
    for copy in planes:
        copy.start()

    sent = []

    def send(source, target, where):
        place = len(sent)
        copy = pltpu.make_async_remote_copy(
            src_ref=source, dst_ref=target, send_sem=send_sem.at[place],
            recv_sem=recv_sem.at[place], device_id=where, device_id_type=MESH,
        )
        copy.start()
        sent.append(copy)
        return copy

    def blocks(ref):
        return [ref[x, z:z + ROWS, :] for x in range(X) for z in range(0, D, ROWS)]

    pl.semaphore_wait(barrier, len(near))
    sink_in = []
    for side, (edge, dx) in enumerate(((X - 1, 1), (0, -1))):
        sink_in.append(send(temp_ref.at[edge], sx_in.at[side, 0], device(dx, 0, 0)))
        sink_in.append(send(diff_ref.at[edge], sx_in.at[side, 1], device(dx, 0, 0)))

    def collide_plane(step, carry):
        x = lax.rem(step + X - 1, X)
        pltpu.make_async_copy(pops_ref.at[:, x], pops.at[:, x], load_sem.at[x]).wait()
        for z in range(0, Z, ROWS):
            for y in range(0, Y, LANES):
                tile = [pops[i, x, z:z + ROWS, y:y + LANES] for i in range(COUNT)]
                done, square = collide(tile)
                for i in range(COUNT):
                    post[SLOT[i], x, z:z + ROWS, y:y + LANES] = done[i]
                if z == 0:
                    heat[x, :, y:y + LANES] = H_BASE + H_GAIN * square
        return carry

    face_in, edge_in, flank_edge_in = [], [], []
    lax.fori_loop(0, 2, collide_plane, 0)
    ends = ((X - 1, 1), (0, -1))
    for side, (edge, dx) in enumerate(ends):
        face_in.append(send(
            post.at[SLOT[INDEX[(dx, 0, 0)]], edge], px_in.at[side, 0], device(dx, 0, 0)
        ))
    lax.fori_loop(2, X, collide_plane, 0)

    for side, (lane, dy) in enumerate(((Y - LANES, 1), (0, -1))):
        tiles = [
            post[SLOT[INDEX[(a, dy, c)]], x, z:z + ROWS, lane:lane + LANES]
            for a, c in ACROSS for x in range(X) for z in range(0, Z, ROWS)
        ]
        py_out[side] = edge_pack(tiles, dy == 1)
        flank_edge_in.append(send(py_out.at[side], py_in.at[side], device(0, dy, 0)))
    for k, (a, b) in enumerate(ACROSS):
        for x in range(X):
            row = jnp.where(
                lowest,
                post[SLOT[INDEX[(a, b, 1)]], x, Z - 1:Z, :],
                post[SLOT[INDEX[(a, b, -1)]], x, 0:1, :],
            )
            pz_out[k * X + x:k * X + x + 1, :] = row
            if b == 1:
                yz_out[0, x:x + 1, :] = row[:, Y - LANES:]
            if b == -1:
                yz_out[1, x:x + 1, :] = row[:, :LANES]
    edge_in.append(send(pz_out, pz_in, device(0, 0, 1)))
    for side, s in enumerate((1, -1)):
        edge_in.append(send(yz_out.at[side], yz_in.at[side], device(0, s, 1)))

    for x in range(X):
        heat_out[x:x + 1, :] = heat[x, 0:1, W:2 * W]
    heat_copy = send(heat_out, heat_in, device(0, 0, 1))

    lane = lanes_like((D, W))
    depth = rows_like((D, W))
    depth_blocks = D // ROWS
    column = depth_blocks * X

    def beside(value, packs, x, start):
        places = range(start + x * depth_blocks, start + (x + 1) * depth_blocks)
        low = jnp.where(lane == 0, edge_column(packs[0], places, False), turned(value, 1, 1))
        high = jnp.where(
            lane == W - 1, edge_column(packs[1], places, True), turned(value, -1, 1)
        )
        return low, high

    def sweep_first(x):
        own, cond = temp[x], 0.5 * diff[x]
        below = (temp[x - 1], diff[x - 1]) if x > 0 else (sx_in[0, 0], sx_in[0, 1])
        above = (temp[x + 1], diff[x + 1]) if x < X - 1 else (sx_in[1, 0], sx_in[1, 1])
        temps = [below[0], above[0], *beside(own, (sy_in[0], sy_in[1]), x, 0)]
        conds = [0.5 * below[1], 0.5 * above[1], *beside(cond, (sy_in[0], sy_in[1]), x, column)]
        g = [cond + c for c in conds]
        g.append(jnp.where(depth == D - 1, 0.0, cond + turned(cond, -1, 0)))
        g.append(jnp.where(depth == 0, 0.0, cond + turned(cond, 1, 0)))
        temps += [turned(own, -1, 0), turned(own, 1, 0)]
        warm = jnp.where(lowest, heat[x, 0:1, 0:W], heat_in[x:x + 1, :])
        start = own + jnp.where(depth == 0, load_ref[x:x + 1, :], 0.0)
        start = start + jnp.where(depth == D - 1, warm * cool_ref[x:x + 1, :], 0.0)
        denom = 1.0 + jnp.where(depth == D - 1, warm, 0.0)
        numer = start
        for k in range(6):
            numer = numer + g[k] * temps[k]
            denom = denom + g[k]
            links[k, x] = g[k]
        flip = 1.0 / denom
        base[x] = start
        inverse[x] = flip
        first[x] = numer * flip
    wide = lanes_like((Z, Y))
    flat = lanes_like((1, Y))
    level = rows_like((Z, Y))

    def shifted(value, lanes, border, b):
        parts = [border, value[:, LANES:]] if b == 1 else [value[:, :Y - LANES], border]
        edge = jnp.concatenate(parts, axis=1)
        spot = 0 if b == 1 else Y - 1
        return jnp.where(lanes == spot, edge, turned(value, b, 1))

    tall = Z // ROWS

    floor = level == jnp.where(lowest, 0, -1)
    roof = level == jnp.where(lowest, -1, Z - 1)

    def move(i, source):
        a, b, c = VELOCITIES[i]
        value = post[SLOT[i], source]
        if b != 0:
            flank = 0 if b == 1 else 1
            begin = (ACROSS.index((a, c)) * X + source) * tall
            border = edge_column(py_in[flank], range(begin, begin + tall), b == -1)
            value = shifted(value, wide, border, b)
        if c != 0:
            at = ACROSS.index((a, b)) * X + source
            row = pz_in[at:at + 1, :]
            if b != 0:
                row = shifted(row, flat, turned(yz_in[flank], b, 1)[source:source + 1, :], b)
            value = jnp.where(level == (0 if c == 1 else Z - 1), row, turned(value, c, 0))
        return value

    def assemble(x, members):
        nozzle = nozzle_ref[x:x + 1, :] == 1
        outlet = wall_ref[x:x + 1, :] == 1
        for i in members:
            a, b, c = VELOCITIES[i]
            if 0 <= x - a < X:
                value = move(i, x - a)
            else:
                side = 0 if a == 1 else 1
                value = px_in[side, SLOT[i] - side * FACE]
            back = SLOT[OPPOSITE[i]]
            if c == 1:
                value = jnp.where(floor, post[back, x, 0:1, :], value)
            if c == -1:
                closed = post[back, x, Z - 1:Z, :]
                jet = closed + 6.0 * WEIGHTS[i] * JET_SPEED
                plate = jnp.where(
                    nozzle, jet, jnp.where(outlet, post[SLOT[i], x, Z - 1:Z, :], closed)
                )
                value = jnp.where(roof, plate, value)
            out_ref[i, x] = value

    def sweep_second(x):
        own = first[x]
        below = first[x - 1] if x > 0 else fx_in[0]
        above = first[x + 1] if x < X - 1 else fx_in[1]
        sides = beside(own, (fy_in[0], fy_in[1]), x, 0)
        temps = [below, above, *sides, turned(own, -1, 0), turned(own, 1, 0)]
        numer = base[x]
        for k in range(6):
            numer = numer + links[k, x] * temps[k]
        solid_ref[x] = numer * inverse[x]

    inner = range(1, X - 1)
    own = {x: [i for i in range(COUNT) if 0 <= x - VELOCITIES[i][0] < X] for x in range(X)}
    def send_face(first_one, last_one):
        for side, (edge, dx) in enumerate(ends):
            for k in range(first_one, last_one):
                px_out[side, k] = move(ORDER[side * FACE + k], edge)
            part = pl.ds(first_one, last_one - first_one)
            face_in.append(
                send(px_out.at[side, part], px_in.at[side, part], device(dx, 0, 0))
            )

    for copy in flank_edge_in:
        copy.wait_recv()
    send_face(1, 3)
    for copy in loads:
        copy.wait()
    halved = [0.5 * tile for tile in blocks(diff)]
    sy_out[0] = edge_pack(blocks(temp) + halved, True)
    flank_in = [send(sy_out.at[0], sy_in.at[0], ahead)]
    sy_out[1] = edge_pack(blocks(temp) + halved, False)
    flank_in.append(send(sy_out.at[1], sy_in.at[1], behind))

    for copy in edge_in:
        copy.wait_recv()
    send_face(3, FACE)
    for copy in planes:
        copy.wait()
    for copy in flank_in + [heat_copy]:
        copy.wait_recv()
    for x in inner:
        sweep_first(x)
    for copy in sink_in:
        copy.wait_recv()
    first_in = []
    for side, (edge, dx) in enumerate(((X - 1, 1), (0, -1))):
        sweep_first(edge)
        first_in.append(send(first.at[edge], fx_in.at[side], device(dx, 0, 0)))
    fy_out[0] = edge_pack(blocks(first), True)
    beside_in = [send(fy_out.at[0], fy_in.at[0], ahead)]
    fy_out[1] = edge_pack(blocks(first), False)
    beside_in.append(send(fy_out.at[1], fy_in.at[1], behind))
    for x in range(X):
        assemble(x, own[x])
    for copy in beside_in:
        copy.wait_recv()
    for x in inner:
        sweep_second(x)
    for copy in first_in:
        copy.wait_recv()
    sweep_second(0)
    sweep_second(X - 1)
    for copy in face_in:
        copy.wait_recv()
    for x in (0, X - 1):
        assemble(x, [i for i in range(COUNT) if i not in own[x]])
    for copy in sent:
        copy.wait_send()


def body(populations, nozzle_mask, wall_type, solid_temp, diffusion, heat_load, coolant_temp):
    sizes = tuple(lax.axis_size(name) for name in ("gx", "gy", "gz"))
    assert sizes[0] > 1 and sizes[1] > 1 and sizes[2] == 2
    _, X, Z, Y = populations.shape
    _, D, W = solid_temp.shape
    assert X >= 2 and W == LANES and Y == sizes[2] * W and Z % ROWS == 0 and D % ROWS == 0
    assert 2 * X * (D // ROWS) <= LANES and len(ACROSS) * X * (Z // ROWS) <= LANES
    rows = -(-len(ACROSS) * X // ROWS) * ROWS
    tall = -(-X // ROWS) * ROWS

    def vmem(*shape):
        return pltpu.VMEM(shape, jnp.float32)

    pair = vmem(2, ROWS, LANES)
    scratch = [
        pltpu.VMEM((X, Y), jnp.int32), pltpu.VMEM((X, Y), jnp.int32), vmem(X, W), vmem(X, W),
        vmem(COUNT, X, Z, Y), vmem(COUNT, X, Z, Y),
        vmem(X, D, W), vmem(X, D, W), vmem(X, D, W),
        vmem(6, X, D, W), vmem(X, D, W), vmem(X, D, W),
        vmem(X, ROWS, Y),
        vmem(2, 2, D, W), pair, pair,
        vmem(tall, W), vmem(tall, W),
        vmem(2, FACE, Z, Y), vmem(2, FACE, Z, Y), pair, pair,
        vmem(rows, Y), vmem(rows, Y),
        vmem(2, tall, LANES), vmem(2, tall, LANES),
        vmem(2, D, W), pair, pair,
        pltpu.SemaphoreType.DMA((X + 6,)),
        pltpu.SemaphoreType.DMA((22,)),
        pltpu.SemaphoreType.DMA((22,)),
    ]
    far = pl.BlockSpec(memory_space=pltpu.HBM)
    local = pl.BlockSpec(memory_space=pltpu.VMEM)
    moved, swept = pl.pallas_call(
        functools.partial(kernel, sizes),
        out_shape=(
            pltpu.VMEM(populations.shape, jnp.float32),
            pltpu.VMEM(solid_temp.shape, jnp.float32),
        ),
        in_specs=[far] * 7,
        out_specs=[local, local],
        scratch_shapes=scratch,
        compiler_params=pltpu.CompilerParams(
            collective_id=0, has_side_effects=True, vmem_limit_bytes=24 * 1024 * 1024
        ),
    )(*(
        pltpu.with_memory_space_constraint(value, pltpu.HBM)
        for value in (populations, solid_temp, diffusion, nozzle_mask, wall_type, heat_load,
                      coolant_temp)
    ))
    return pl.pallas_call(
        deliver,
        out_shape=(
            pltpu.HBM(populations.shape, jnp.float32),
            pltpu.HBM(solid_temp.shape, jnp.float32),
        ),
        in_specs=[pl.BlockSpec(memory_space=pl.ANY)] * 2,
        out_specs=[far, far],
        scratch_shapes=[pltpu.SemaphoreType.DMA((2,))],
        compiler_params=pltpu.CompilerParams(vmem_limit_bytes=1024 * 1024),
    )(*(pltpu.with_memory_space_constraint(value, pltpu.VMEM) for value in (moved, swept)))


def deliver(moved_ref, swept_ref, out_ref, solid_ref, sem):
    copies = [
        pltpu.make_async_copy(moved_ref, out_ref, sem.at[0]),
        pltpu.make_async_copy(swept_ref, solid_ref, sem.at[1]),
    ]
    for copy in copies:
        copy.start()
    for copy in copies:
        copy.wait()


def solution(mesh):
    placed = (
        P(None, "gx", "gz", "gy"),
        P("gx", "gy"),
        P("gx", "gy"),
        P("gx", None, ("gy", "gz")),
        P("gx", None, ("gy", "gz")),
        P("gx", ("gy", "gz")),
        P("gx", ("gy", "gz")),
    )
    return jax.shard_map(
        body,
        mesh=mesh,
        in_specs=placed,
        out_specs=(P(None, "gx", "gz", "gy"), P("gx", None, ("gy", "gz"))),
        check_vma=False,
    )
```

```python
import functools
import jax
import jax.numpy as jnp
import numpy as np
from jax import lax
from jax.experimental import pallas as pl
from jax.experimental.pallas import tpu as pltpu
from jax.sharding import PartitionSpec as P

JET_SPEED = 0.1
H_BASE = 0.5
H_GAIN = 40.0
LANES = 128
ROWS = 8
MESH = pl.DeviceIdType.MESH

VELOCITIES = [
    (0, 0, 0),
    (1, 0, 0), (-1, 0, 0), (0, 1, 0), (0, -1, 0), (0, 0, 1), (0, 0, -1),
    (1, 1, 0), (-1, -1, 0), (1, -1, 0), (-1, 1, 0),
    (1, 0, 1), (-1, 0, -1), (1, 0, -1), (-1, 0, 1),
    (0, 1, 1), (0, -1, -1), (0, 1, -1), (0, -1, 1),
]
COUNT = len(VELOCITIES)
WEIGHTS = [1.0 / 3.0] + [1.0 / 18.0] * 6 + [1.0 / 36.0] * 12
INDEX = {velocity: member for member, velocity in enumerate(VELOCITIES)}
OPPOSITE = [INDEX[(-a, -b, -c)] for a, b, c in VELOCITIES]
ORDER = [i for s in (1, -1, 0) for i in range(COUNT) if VELOCITIES[i][0] == s]
SLOT = {member: place for place, member in enumerate(ORDER)}
FACE = sum(1 for v in VELOCITIES if v[0] == 1)
ACROSS = [(0, 0), (1, 0), (-1, 0), (0, 1), (0, -1)]


def collide(f):
    s = {i: f[i] + f[i + 1] for i in range(1, COUNT, 2)}
    d = {i: f[i] - f[i + 1] for i in range(1, COUNT, 2)}
    jx = (d[1] + d[7]) + (d[9] + d[11]) + d[13]
    jy = (d[3] + d[7]) + (d[15] - d[9]) + d[17]
    jz = (d[5] + d[11]) + (d[15] - d[13]) - d[17]
    sxy, sxz, syz = s[7] + s[9], s[11] + s[13], s[15] + s[17]
    rho = f[0] + (s[1] + s[3] + s[5]) + (sxy + sxz + syz)
    inv = 1.0 / rho
    ux, uy, uz = jx * inv, jy * inv, jz * inv
    px, py, pz = jx * ux, jy * uy, jz * uz
    p = px + py + pz
    base = rho - 1.5 * p
    hxy, hxz, hyz = px + py, px + pz, py + pz
    c4 = 4.0 * f[0] - base
    qxy = c4 + sxy - 2.0 * (s[1] + s[3]) + 0.5 * hxy
    qxz = c4 + sxz - 2.0 * (s[1] + s[5]) + 0.5 * hxz
    qyz = c4 + syz - 2.0 * (s[3] + s[5]) + 0.5 * hyz
    mean = (qxy + qxz + qyz) * (2.0 / 7.0)
    txy, txz, tyz = ((q - mean) * (0.2 / 12.0) for q in (qxy, qxz, qyz))
    post = [None] * COUNT
    post[0] = (1.6 / 3.0) * base - 0.6 * f[0] + 4.0 * (txy + txz + tyz)
    axis_base = (1.6 / 18.0) * base
    for i, pp, tt, j in ((1, px, txy + txz, jx), (3, py, txy + tyz, jy), (5, pz, txz + tyz, jz)):
        even = axis_base + 0.4 * pp - 0.3 * s[i] - 2.0 * tt
        odd = 0.2 * j - 0.1 * d[i]
        post[i], post[i + 1] = even + odd, even - odd
    diag_base = (1.6 / 36.0) * base
    for i, hh, tt, j, k, u in (
        (7, hxy, txy, jx, jy, uy), (11, hxz, txz, jx, jz, uz), (15, hyz, tyz, jy, jz, uz)
    ):
        both = diag_base + 0.2 * hh + tt
        cross = 0.4 * (j * u)
        even = both + cross - 0.3 * s[i]
        odd = 0.1 * (j + k - d[i])
        post[i], post[i + 1] = even + odd, even - odd
        even = both - cross - 0.3 * s[i + 2]
        odd = 0.1 * (j - k - d[i + 2])
        post[i + 2], post[i + 3] = even + odd, even - odd
    return post, p * inv


def lanes_like(shape):
    return lax.broadcasted_iota(jnp.int32, shape, len(shape) - 1)


def rows_like(shape):
    return lax.broadcasted_iota(jnp.int32, shape, len(shape) - 2)


def turned(value, shift, axis):
    shift = shift % value.shape[axis]
    return value if shift == 0 else pltpu.roll(value, shift, axis)


def edge_pack(tiles, last):
    lane = lanes_like((ROWS, LANES))
    packed = jnp.zeros((ROWS, LANES), jnp.float32)
    for k, tile in enumerate(tiles):
        packed = jnp.where(lane == k, turned(tile, k + 1 if last else k, 1), packed)
    return packed


def edge_column(packed, places, last):
    return jnp.concatenate(
        [turned(packed, (LANES - 1 if last else 0) - k, 1) for k in places], axis=0
    )


def kernel(sizes, pops_ref, temp_ref, diff_ref, nozzle_hbm, wall_hbm, load_hbm, cool_hbm,
           out_ref, solid_ref, nozzle_ref, wall_ref, load_ref, cool_ref, pops, post, temp, diff, first, links, base, inverse, heat,
           sx_in, sy_out, sy_in, heat_out, heat_in, px_out, px_in, py_out, py_in, pz_out, pz_in,
           yz_out, yz_in, fx_in, fy_out, fy_in,
           load_sem, send_sem, recv_sem):
    nx, ny, nz = sizes
    gx, gy, gz = (lax.axis_index(name) for name in ("gx", "gy", "gz"))
    X, Z, Y = pops.shape[1:]
    D, W = temp.shape[1:]
    lowest = gz == 0

    def device(dx, dy, other):
        return (lax.rem(gx + dx + nx, nx), lax.rem(gy + dy + ny, ny), 1 - gz if other else gz)

    ahead = (gx, lax.rem(gy + gz, ny), 1 - gz)
    behind = (gx, lax.rem(gy + gz - 1 + ny, ny), 1 - gz)

    near = set()
    for dx, dy, other in (
        [(s, 0, 0) for s in (1, -1)] + [(0, s, 0) for s in (1, -1)] + [(0, 0, 1)]
        + [(0, s, 1) for s in (1, -1)]
    ):
        near.add((dx % nx, dy % ny, other))
    barrier = pltpu.get_barrier_semaphore()
    for dx, dy, other in sorted(near):
        pl.semaphore_signal(
            barrier, inc=1, device_id=device(dx, dy, other), device_id_type=MESH
        )

    loads = [
        pltpu.make_async_copy(temp_ref, temp, load_sem.at[X]),
        pltpu.make_async_copy(diff_ref, diff, load_sem.at[X + 1]),
    ]
    planes = [
        pltpu.make_async_copy(far, near_by, load_sem.at[X + 2 + k])
        for k, (far, near_by) in enumerate((
            (nozzle_hbm, nozzle_ref), (wall_hbm, wall_ref),
            (load_hbm, load_ref), (cool_hbm, cool_ref),
        ))
    ]
    for copy in loads:
        copy.start()
    turn = [X - 1] + list(range(X - 1))
    for x in turn:
        pltpu.make_async_copy(pops_ref.at[:, x], pops.at[:, x], load_sem.at[x]).start()
    for copy in planes:
        copy.start()

    sent = []

    def send(source, target, where):
        place = len(sent)
        copy = pltpu.make_async_remote_copy(
            src_ref=source, dst_ref=target, send_sem=send_sem.at[place],
            recv_sem=recv_sem.at[place], device_id=where, device_id_type=MESH,
        )
        copy.start()
        sent.append(copy)
        return copy

    def blocks(ref):
        return [ref[x, z:z + ROWS, :] for x in range(X) for z in range(0, D, ROWS)]

    pl.semaphore_wait(barrier, len(near))
    sink_in = []
    for side, (edge, dx) in enumerate(((X - 1, 1), (0, -1))):
        sink_in.append(send(temp_ref.at[edge], sx_in.at[side, 0], device(dx, 0, 0)))
        sink_in.append(send(diff_ref.at[edge], sx_in.at[side, 1], device(dx, 0, 0)))

    for copy in loads:
        copy.wait()
    halved = [0.5 * tile for tile in blocks(diff)]
    sy_out[0] = edge_pack(blocks(temp) + halved, True)
    flank_in = [send(sy_out.at[0], sy_in.at[0], ahead)]
    sy_out[1] = edge_pack(blocks(temp) + halved, False)
    flank_in.append(send(sy_out.at[1], sy_in.at[1], behind))

    def collide_plane(step, carry):
        x = lax.rem(step + X - 1, X)
        pltpu.make_async_copy(pops_ref.at[:, x], pops.at[:, x], load_sem.at[x]).wait()
        for z in range(0, Z, ROWS):
            for y in range(0, Y, LANES):
                tile = [pops[i, x, z:z + ROWS, y:y + LANES] for i in range(COUNT)]
                done, square = collide(tile)
                for i in range(COUNT):
                    post[SLOT[i], x, z:z + ROWS, y:y + LANES] = done[i]
                if z == 0:
                    heat[x, :, y:y + LANES] = H_BASE + H_GAIN * square
        return carry

    lax.fori_loop(0, X, collide_plane, 0)
    face_in, edge_in = [], []

    for x in range(X):
        heat_out[x:x + 1, :] = heat[x, 0:1, W:2 * W]
    heat_copy = send(heat_out, heat_in, device(0, 0, 1))

    for side, (lane, dy) in enumerate(((Y - LANES, 1), (0, -1))):
        tiles = [
            post[SLOT[INDEX[(a, dy, c)]], x, z:z + ROWS, lane:lane + LANES]
            for a, c in ACROSS for x in range(X) for z in range(0, Z, ROWS)
        ]
        py_out[side] = edge_pack(tiles, dy == 1)
        edge_in.append(send(py_out.at[side], py_in.at[side], device(0, dy, 0)))
    for k, (a, b) in enumerate(ACROSS):
        for x in range(X):
            row = jnp.where(
                lowest,
                post[SLOT[INDEX[(a, b, 1)]], x, Z - 1:Z, :],
                post[SLOT[INDEX[(a, b, -1)]], x, 0:1, :],
            )
            pz_out[k * X + x:k * X + x + 1, :] = row
            if b == 1:
                yz_out[0, x:x + 1, :] = row[:, Y - LANES:]
            if b == -1:
                yz_out[1, x:x + 1, :] = row[:, :LANES]
    edge_in.append(send(pz_out, pz_in, device(0, 0, 1)))
    for side, s in enumerate((1, -1)):
        edge_in.append(send(yz_out.at[side], yz_in.at[side], device(0, s, 1)))

    lane = lanes_like((D, W))
    depth = rows_like((D, W))
    depth_blocks = D // ROWS
    column = depth_blocks * X

    def beside(value, packs, x, start):
        places = range(start + x * depth_blocks, start + (x + 1) * depth_blocks)
        low = jnp.where(lane == 0, edge_column(packs[0], places, False), turned(value, 1, 1))
        high = jnp.where(
            lane == W - 1, edge_column(packs[1], places, True), turned(value, -1, 1)
        )
        return low, high

    def sweep_first(x):
        own, cond = temp[x], 0.5 * diff[x]
        below = (temp[x - 1], diff[x - 1]) if x > 0 else (sx_in[0, 0], sx_in[0, 1])
        above = (temp[x + 1], diff[x + 1]) if x < X - 1 else (sx_in[1, 0], sx_in[1, 1])
        temps = [below[0], above[0], *beside(own, (sy_in[0], sy_in[1]), x, 0)]
        conds = [0.5 * below[1], 0.5 * above[1], *beside(cond, (sy_in[0], sy_in[1]), x, column)]
        g = [cond + c for c in conds]
        g.append(jnp.where(depth == D - 1, 0.0, cond + turned(cond, -1, 0)))
        g.append(jnp.where(depth == 0, 0.0, cond + turned(cond, 1, 0)))
        temps += [turned(own, -1, 0), turned(own, 1, 0)]
        warm = jnp.where(lowest, heat[x, 0:1, 0:W], heat_in[x:x + 1, :])
        start = own + jnp.where(depth == 0, load_ref[x:x + 1, :], 0.0)
        start = start + jnp.where(depth == D - 1, warm * cool_ref[x:x + 1, :], 0.0)
        denom = 1.0 + jnp.where(depth == D - 1, warm, 0.0)
        numer = start
        for k in range(6):
            numer = numer + g[k] * temps[k]
            denom = denom + g[k]
            links[k, x] = g[k]
        flip = 1.0 / denom
        base[x] = start
        inverse[x] = flip
        first[x] = numer * flip
    wide = lanes_like((Z, Y))
    flat = lanes_like((1, Y))
    level = rows_like((Z, Y))

    def shifted(value, lanes, border, b):
        parts = [border, value[:, LANES:]] if b == 1 else [value[:, :Y - LANES], border]
        edge = jnp.concatenate(parts, axis=1)
        spot = 0 if b == 1 else Y - 1
        return jnp.where(lanes == spot, edge, turned(value, b, 1))

    tall = Z // ROWS

    floor = level == jnp.where(lowest, 0, -1)
    roof = level == jnp.where(lowest, -1, Z - 1)

    def move(i, source):
        a, b, c = VELOCITIES[i]
        value = post[SLOT[i], source]
        if b != 0:
            flank = 0 if b == 1 else 1
            begin = (ACROSS.index((a, c)) * X + source) * tall
            border = edge_column(py_in[flank], range(begin, begin + tall), b == -1)
            value = shifted(value, wide, border, b)
        if c != 0:
            at = ACROSS.index((a, b)) * X + source
            row = pz_in[at:at + 1, :]
            if b != 0:
                row = shifted(row, flat, turned(yz_in[flank], b, 1)[source:source + 1, :], b)
            value = jnp.where(level == (0 if c == 1 else Z - 1), row, turned(value, c, 0))
        return value

    def assemble(x, members):
        nozzle = nozzle_ref[x:x + 1, :] == 1
        outlet = wall_ref[x:x + 1, :] == 1
        for i in members:
            a, b, c = VELOCITIES[i]
            if 0 <= x - a < X:
                value = move(i, x - a)
            else:
                side = 0 if a == 1 else 1
                value = px_in[side, SLOT[i] - side * FACE]
            back = SLOT[OPPOSITE[i]]
            if c == 1:
                value = jnp.where(floor, post[back, x, 0:1, :], value)
            if c == -1:
                closed = post[back, x, Z - 1:Z, :]
                jet = closed + 6.0 * WEIGHTS[i] * JET_SPEED
                plate = jnp.where(
                    nozzle, jet, jnp.where(outlet, post[SLOT[i], x, Z - 1:Z, :], closed)
                )
                value = jnp.where(roof, plate, value)
            out_ref[i, x] = value

    def sweep_second(x):
        own = first[x]
        below = first[x - 1] if x > 0 else fx_in[0]
        above = first[x + 1] if x < X - 1 else fx_in[1]
        sides = beside(own, (fy_in[0], fy_in[1]), x, 0)
        temps = [below, above, *sides, turned(own, -1, 0), turned(own, 1, 0)]
        numer = base[x]
        for k in range(6):
            numer = numer + links[k, x] * temps[k]
        solid_ref[x] = numer * inverse[x]

    inner = range(1, X - 1)
    own = {x: [i for i in range(COUNT) if 0 <= x - VELOCITIES[i][0] < X] for x in range(X)}
    for copy in planes:
        copy.wait()
    for copy in flank_in + [heat_copy] + sink_in:
        copy.wait_recv()
    first_in = []
    for side, (edge, dx) in enumerate(((X - 1, 1), (0, -1))):
        sweep_first(edge)
        first_in.append(send(first.at[edge], fx_in.at[side], device(dx, 0, 0)))
    for copy in edge_in:
        copy.wait_recv()
    for side, (edge, dx) in enumerate(((X - 1, 1), (0, -1))):
        for k in range(FACE):
            px_out[side, k] = move(ORDER[side * FACE + k], edge)
        face_in.append(send(px_out.at[side], px_in.at[side], device(dx, 0, 0)))
    for x in inner:
        sweep_first(x)
    fy_out[0] = edge_pack(blocks(first), True)
    beside_in = [send(fy_out.at[0], fy_in.at[0], ahead)]
    fy_out[1] = edge_pack(blocks(first), False)
    beside_in.append(send(fy_out.at[1], fy_in.at[1], behind))
    for x in range(X):
        assemble(x, own[x])
    for copy in beside_in:
        copy.wait_recv()
    for x in inner:
        sweep_second(x)
    for copy in first_in:
        copy.wait_recv()
    sweep_second(0)
    sweep_second(X - 1)
    for copy in face_in:
        copy.wait_recv()
    for x in (0, X - 1):
        assemble(x, [i for i in range(COUNT) if i not in own[x]])
    for copy in sent:
        copy.wait_send()


def body(populations, nozzle_mask, wall_type, solid_temp, diffusion, heat_load, coolant_temp):
    sizes = tuple(lax.axis_size(name) for name in ("gx", "gy", "gz"))
    assert sizes[0] > 1 and sizes[1] > 1 and sizes[2] == 2
    _, X, Z, Y = populations.shape
    _, D, W = solid_temp.shape
    assert X >= 2 and W == LANES and Y == sizes[2] * W and Z % ROWS == 0 and D % ROWS == 0
    assert 2 * X * (D // ROWS) <= LANES and len(ACROSS) * X * (Z // ROWS) <= LANES
    rows = -(-len(ACROSS) * X // ROWS) * ROWS
    tall = -(-X // ROWS) * ROWS

    def vmem(*shape):
        return pltpu.VMEM(shape, jnp.float32)

    pair = vmem(2, ROWS, LANES)
    scratch = [
        pltpu.VMEM((X, Y), jnp.int32), pltpu.VMEM((X, Y), jnp.int32), vmem(X, W), vmem(X, W),
        vmem(COUNT, X, Z, Y), vmem(COUNT, X, Z, Y),
        vmem(X, D, W), vmem(X, D, W), vmem(X, D, W),
        vmem(6, X, D, W), vmem(X, D, W), vmem(X, D, W),
        vmem(X, ROWS, Y),
        vmem(2, 2, D, W), pair, pair,
        vmem(tall, W), vmem(tall, W),
        vmem(2, FACE, Z, Y), vmem(2, FACE, Z, Y), pair, pair,
        vmem(rows, Y), vmem(rows, Y),
        vmem(2, tall, LANES), vmem(2, tall, LANES),
        vmem(2, D, W), pair, pair,
        pltpu.SemaphoreType.DMA((X + 6,)),
        pltpu.SemaphoreType.DMA((18,)),
        pltpu.SemaphoreType.DMA((18,)),
    ]
    far = pl.BlockSpec(memory_space=pltpu.HBM)
    local = pl.BlockSpec(memory_space=pltpu.VMEM)
    moved, swept = pl.pallas_call(
        functools.partial(kernel, sizes),
        out_shape=(
            pltpu.VMEM(populations.shape, jnp.float32),
            pltpu.VMEM(solid_temp.shape, jnp.float32),
        ),
        in_specs=[far] * 7,
        out_specs=[local, local],
        scratch_shapes=scratch,
        compiler_params=pltpu.CompilerParams(
            collective_id=0, has_side_effects=True, vmem_limit_bytes=24 * 1024 * 1024
        ),
    )(*(
        pltpu.with_memory_space_constraint(value, pltpu.HBM)
        for value in (populations, solid_temp, diffusion, nozzle_mask, wall_type, heat_load,
                      coolant_temp)
    ))
    return pl.pallas_call(
        deliver,
        out_shape=(
            pltpu.HBM(populations.shape, jnp.float32),
            pltpu.HBM(solid_temp.shape, jnp.float32),
        ),
        in_specs=[pl.BlockSpec(memory_space=pl.ANY)] * 2,
        out_specs=[far, far],
        scratch_shapes=[pltpu.SemaphoreType.DMA((2,))],
        compiler_params=pltpu.CompilerParams(vmem_limit_bytes=1024 * 1024),
    )(*(pltpu.with_memory_space_constraint(value, pltpu.VMEM) for value in (moved, swept)))


def deliver(moved_ref, swept_ref, out_ref, solid_ref, sem):
    copies = [
        pltpu.make_async_copy(moved_ref, out_ref, sem.at[0]),
        pltpu.make_async_copy(swept_ref, solid_ref, sem.at[1]),
    ]
    for copy in copies:
        copy.start()
    for copy in copies:
        copy.wait()


def solution(mesh):
    placed = (
        P(None, "gx", "gz", "gy"),
        P("gx", "gy"),
        P("gx", "gy"),
        P("gx", None, ("gy", "gz")),
        P("gx", None, ("gy", "gz")),
        P("gx", ("gy", "gz")),
        P("gx", ("gy", "gz")),
    )
    return jax.shard_map(
        body,
        mesh=mesh,
        in_specs=placed,
        out_specs=(P(None, "gx", "gz", "gy"), P("gx", None, ("gy", "gz"))),
        check_vma=False,
    )
```
